256 devices in a mesh: gx: 8 (over x, core), gy: 32 (over y, z).
Axes of the slice: x: 4, y: 4, z: 8, core: 2. Of those that a mesh axis runs over, the one named last changes fastest.
Arguments:
- field: bfloat16 [128, 128, 20, 1024], P('gx', 'gy'), may hold values from -6 to 6
- cotangent: bfloat16 [128, 128, 20, 1024], P('gx', 'gy'), may hold values from -6 to 6
- spectral_weight: float32 [2, 20, 20, 24, 24, 96], P(None, None, None, None, 'gx', 'gy'), may hold values from -16 to 16
- pointwise_weight: bfloat16 [20, 20], replicated, may hold values from -1.25 to 1.25
- channel_bias: float32 [20], replicated, may hold values from -3 to 3
Outputs:
- output: bfloat16 [128, 128, 20, 1024], P('gx', 'gy')
- grad_field: bfloat16 [128, 128, 20, 1024], P('gx', 'gy')
- grad_weight: float32 [2, 20, 20, 24, 24, 96], P(None, None, None, None, 'gx', 'gy')
The draws below stay inside these ranges and needn't reach their ends.
All inputs are finite; a program needn't handle non-finite values.
Results may differ from the reference program's by a relative error of at most 0.0054.
Values sent between devices are 32-bit elements; how exact they have to be, the bound alone decides.
No kernel may reach another device: no remote copies, remote signals or barrier semaphores. Data moves between devices by JAX's collectives and lax.ppermute only.
A program may use at most 192 MiB of HBM per device.

```python
import math
import jax
import jax.numpy as jnp
from jax import lax

NX = 128
NY = 128
NZ = 64
NT = 16
C = 20
KX = 24
KY = 24
KZ = 12
KT = 8


def steps_of(key, dims, shards, low, top_value):
    factor_of = 1.0
    for axis_at, blocks in shards:
        draws = jax.random.uniform(jax.random.fold_in(jax.random.fold_in(key, 6), axis_at), (blocks,), jnp.float32, low / len(shards), top_value / len(shards))
        factor_of = factor_of * jnp.repeat(jnp.exp(draws), dims[axis_at] // blocks).reshape((-1,) + (1,) * (len(dims) - 1 - axis_at))
    return factor_of


def normal_values(own_key, dims, scale, most, pieces=(), kind=jnp.bfloat16):
    drawn = jax.random.normal(own_key, dims, jnp.float32) * scale
    if len(pieces) > 0:
        drawn = steps_of(own_key, dims, pieces, -0.22, 0.18) * drawn
    return jnp.clip(drawn, min=-most, max=most).astype(kind)


def setup_inputs(seed: int = 0) -> dict:
    splits = jax.random.split(jax.random.key(seed), 6)
    field = normal_values(splits[0], (NX, NY, C, NZ * NT), 1.0, 6.0, ((0, 8), (1, 32)))
    cotangent = normal_values(splits[1], (NX, NY, C, NZ * NT), 1.0, 6.0, ((0, 8), (1, 32)))
    spectral_weight = normal_values(splits[2], (2, C, C, KX, KY, KZ * KT), ((NX * NY * NZ * NT) ** 0.5 * (2 * C * KX * KY * KZ * KT) ** -0.5), 16.0, ((4, 8), (5, 32)), jnp.float32)
    pointwise_weight = normal_values(splits[3], (C, C), C ** -0.5, 1.25)
    channel_bias = normal_values(splits[4], (C,), 0.5, 3.0, (), jnp.float32)
    return {"field": field, "cotangent": cotangent, "spectral_weight": spectral_weight, "pointwise_weight": pointwise_weight, "channel_bias": channel_bias}


HIGHEST_PRECISION = lax.Precision.HIGHEST
GELU_SCALE = math.sqrt(2.0 / math.pi)
GELU_CUBIC = 0.044715

def signed_modes(tally_index, modes_total):
    return jnp.where(tally_index < modes_total // 2, tally_index, tally_index - modes_total)

def angle_of(phase, period):
    return phase.astype(jnp.float32) * (2.0 * math.pi / period)

def complex_analysis(positions, period, modes_total):
    frequency = signed_modes(jnp.arange(modes_total, dtype=jnp.int32), modes_total)
    angles = angle_of(jnp.mod(positions[:, None] * frequency[None, :], period), period)
    cosines = jnp.cos(angles)
    sine_part = jnp.sin(angles)
    return jnp.stack([jnp.stack([cosines, -sine_part], axis=1), jnp.stack([sine_part, cosines], axis=1)], axis=0)

def complex_synthesis(positions, period, modes_total):
    frequency = signed_modes(jnp.arange(modes_total, dtype=jnp.int32), modes_total)
    angles = angle_of(jnp.mod(frequency[:, None] * positions[None, :], period), period)
    cosines = jnp.cos(angles) / period
    sine_part = jnp.sin(angles) / period
    return jnp.stack([jnp.stack([cosines, sine_part], axis=1), jnp.stack([-sine_part, cosines], axis=1)], axis=0)

def axis_tables(positions, period, modes_total, forward):
    analysis = complex_analysis(positions, period, modes_total)
    synthesis = complex_synthesis(positions, period, modes_total)
    if forward:
        return (analysis, synthesis)
    return (jnp.transpose(synthesis, (2, 3, 0, 1)), jnp.transpose(analysis, (2, 3, 0, 1)))

def time_angles():
    cells = jnp.arange(NZ * NT, dtype=jnp.int32)
    spectrum_stack = jnp.arange(KZ * KT, dtype=jnp.int32)
    depth_freq = signed_modes(spectrum_stack // KT, KZ)
    time_freq = spectrum_stack % KT
    phase = depth_freq[None, :] * (cells // NT)[:, None] * NT + time_freq[None, :] * (cells % NT)[:, None] * NZ
    return (angle_of(jnp.mod(phase, NZ * NT), NZ * NT), time_freq)

def depth_clock_lookup(forward):
    angles, time_freq = time_angles()
    analysis = jnp.stack([jnp.cos(angles), -jnp.sin(angles)], axis=1)
    weights = jnp.where(time_freq == 0, 1.0, 2.0).astype(jnp.float32) / (NZ * NT)
    synthesis = jnp.stack([jnp.cos(angles).T * weights[:, None], -jnp.sin(angles).T * weights[:, None]], axis=0)
    if forward:
        toward_spectrum, outward = (analysis, synthesis)
    else:
        toward_spectrum, outward = (jnp.transpose(synthesis, (2, 0, 1)), jnp.transpose(analysis, (1, 2, 0)))
    return (toward_spectrum.reshape(NZ * NT, 2 * KZ * KT).astype(jnp.bfloat16), outward)

def contract(spectrum_stack, table, position):
    product = jnp.tensordot(spectrum_stack, table, axes=((0, position), (0, 1)), precision=HIGHEST_PRECISION)
    return jnp.moveaxis(jnp.moveaxis(product, -2, 0), -1, position)

def into_depth_time(spatial_lattice, toward_spectrum):
    product = jnp.dot(spatial_lattice, toward_spectrum, preferred_element_type=jnp.float32)
    shaped = product.reshape(product.shape[:-1] + (2, KZ * KT))
    return jnp.moveaxis(shaped, -2, 0)

def from_depth_time(spectrum_stack, outward):
    return jnp.tensordot(spectrum_stack, outward, axes=((0, spectrum_stack.ndim - 1), (0, 1)), precision=HIGHEST_PRECISION)

def mix_modes(weight, spectrum_stack):
    return jnp.einsum('ioxym,xyim->xyom', weight, spectrum_stack, precision=HIGHEST_PRECISION)

def unmix_modes(weight, spectrum_stack):
    return jnp.einsum('ioxym,xyom->xyim', weight, spectrum_stack, precision=HIGHEST_PRECISION)

def outer_modes(inputs, grads):
    return jnp.einsum('xyim,xyom->ioxym', inputs, grads, precision=HIGHEST_PRECISION)

def spectral_apply(weight, spectrum_stack):
    real_out = mix_modes(weight[0], spectrum_stack[0]) - mix_modes(weight[1], spectrum_stack[1])
    imag_out = mix_modes(weight[0], spectrum_stack[1]) + mix_modes(weight[1], spectrum_stack[0])
    return jnp.stack([real_out, imag_out], axis=0)

def spectral_adjoint(weight, grads):
    real_in = unmix_modes(weight[0], grads[0]) + unmix_modes(weight[1], grads[1])
    imag_in = unmix_modes(weight[0], grads[1]) - unmix_modes(weight[1], grads[0])
    return jnp.stack([real_in, imag_in], axis=0)

def spectral_weight_grad(inputs, grads):
    real_grad = outer_modes(inputs[0], grads[0]) + outer_modes(inputs[1], grads[1])
    imag_grad = outer_modes(inputs[0], grads[1]) - outer_modes(inputs[1], grads[0])
    return jnp.stack([real_grad, imag_grad], axis=0)

def gelu_parts(values):
    inner = GELU_SCALE * (values + GELU_CUBIC * values * values * values)
    tangent = jnp.tanh(inner)
    result = 0.5 * values * (1.0 + tangent)
    slope = 0.5 * (1.0 + tangent) + 0.5 * values * (1.0 - tangent * tangent) * GELU_SCALE * (1.0 + 3.0 * GELU_CUBIC * values * values)
    return (result, slope)

def reference(field, cotangent, spectral_weight, pointwise_weight, channel_bias):
    positions_x = jnp.arange(NX, dtype=jnp.int32)
    positions_y = jnp.arange(NY, dtype=jnp.int32)
    pointwise_wide = pointwise_weight.astype(jnp.float32)

    def finish_analysis(spectrum_stack, forward):
        spectrum_stack = contract(spectrum_stack, axis_tables(positions_y, NY, KY, forward)[0], 2)
        return contract(spectrum_stack, axis_tables(positions_x, NX, KX, forward)[0], 1)

    def synthesize(spectrum_stack, forward):
        spectrum_stack = contract(spectrum_stack, axis_tables(positions_x, NX, KX, forward)[1], 1)
        spectrum_stack = contract(spectrum_stack, axis_tables(positions_y, NY, KY, forward)[1], 2)
        return jnp.moveaxis(spectrum_stack, 1, 0)
    inward_forward, outward_forward = depth_clock_lookup(True)
    inward_backward, outward_backward = depth_clock_lookup(False)

    def analyze_row(grid_row):
        return into_depth_time(grid_row, inward_forward)
    field_rows = lax.map(analyze_row, field)
    field_spectrum = finish_analysis(jnp.moveaxis(field_rows, 1, 0), True)
    mixed_grid = synthesize(spectral_apply(spectral_weight, field_spectrum), True)

    def forward_row(fragment_list):
        spectra_row, field_row, cotangent_row = fragment_list
        spectral_part = from_depth_time(spectra_row, outward_forward)
        linear = jnp.einsum('yiq,io->yoq', field_row.astype(jnp.float32), pointwise_wide, precision=HIGHEST_PRECISION)
        before = spectral_part + linear + channel_bias[None, :, None]
        result, slope = gelu_parts(before)
        pre_grad = (cotangent_row.astype(jnp.float32) * slope).astype(jnp.bfloat16)
        return (result.astype(jnp.bfloat16), pre_grad, into_depth_time(pre_grad, inward_backward))
    output, pre_grads, grad_rows = lax.map(forward_row, (mixed_grid, field, cotangent))
    grad_spectrum = finish_analysis(jnp.moveaxis(grad_rows, 1, 0), False)
    grad_weight = spectral_weight_grad(field_spectrum, grad_spectrum)
    reverse_lattice = synthesize(spectral_adjoint(spectral_weight, grad_spectrum), False)

    def backward_row(fragment_list):
        spectra_row, pre_row = fragment_list
        spectral_part = from_depth_time(spectra_row, outward_backward)
        linear = jnp.einsum('yoq,io->yiq', pre_row.astype(jnp.float32), pointwise_wide, precision=HIGHEST_PRECISION)
        return (spectral_part + linear).astype(jnp.bfloat16)
    grad_field = lax.map(backward_row, (reverse_lattice, pre_grads))
    return (output, grad_field, grad_weight)
```

```python
import math

import jax
import jax.numpy as jnp
import numpy as np
from jax import lax
from jax.experimental import pallas as pl
from jax.experimental.pallas import tpu as pltpu
from jax.sharding import PartitionSpec as P

NX = 128
NY = 128
NZ = 64
NT = 16
C = 20
KX = 24
KY = 24
KZ = 12
KT = 8

GX = 8
GY = 32
XL = NX // GX
YL = NY // GY
KYL = KY // GX
ML = KZ * KT // GY
XC = XL * C
CELLS = XL * C * YL
Q = NZ * NT
N = 2 * ML * GY
LT = 8
G = 4
CG = C // G
KC = CG * KX
MODES = KYL * ML
ROWS = G * 2 * MODES

GELU_SCALE = math.sqrt(2.0 / math.pi)
GELU_CUBIC = 0.044715
F32 = jnp.float32
BF16 = jnp.bfloat16
SCALE = 1.0 / (NX * NY)


def signed(count):
    j = np.arange(count)
    return np.where(j < count // 2, j, j - count)


def halves(table):
    table = np.asarray(table, np.float32)
    high = table.astype(jnp.bfloat16)
    low = (table - high.astype(np.float32)).astype(jnp.bfloat16)
    return high, low


def zt_tables():
    q = np.arange(Q)
    m = (np.arange(GY)[None, :] * ML + np.arange(ML)[:, None]).reshape(-1)
    fz, kt = signed(KZ)[m // KT], m % KT
    phase = (fz[None, :] * (q // NT)[:, None] * NT + kt[None, :] * (q % NT)[:, None] * NZ) % Q
    angles = phase * (2.0 * math.pi / Q)
    weights = np.where(kt == 0, 1.0, 2.0) / Q
    analysis = np.concatenate([np.cos(angles), -np.sin(angles)], axis=1)
    synthesis = analysis * np.concatenate([weights, weights])[None, :]
    return analysis.astype(np.float32), synthesis.astype(np.float32)


def three_rows(table):
    high, low = halves(table)
    return np.concatenate([high, high, low], axis=0)


def y_table():
    ky = (np.arange(GX)[None, :] * KYL + np.arange(KYL)[:, None]).reshape(-1)
    f = signed(KY)[ky]
    n = np.arange(NY)
    angles = ((f[:, None] * n[None, :]) % NY) * (2.0 * math.pi / NY)
    c, s = np.cos(angles), np.sin(angles)
    t = np.zeros((2, KY, GY, 2, YL))
    c4, s4 = c.reshape(KY, GY, YL), s.reshape(KY, GY, YL)
    t[0, :, :, 0], t[0, :, :, 1] = c4, s4
    t[1, :, :, 0], t[1, :, :, 1] = -s4, c4
    return t.reshape(2 * KY, GY * 2 * YL)


def x_table():
    f, x = signed(KX), np.arange(XL)
    angles = ((f[None, :] * x[:, None]) % NX) * (2.0 * math.pi / NX)
    t = np.zeros((XL, C, 2, G, 128))
    for c in range(C):
        g, j = divmod(c, CG)
        t[:, c, 0, g, j * KX : (j + 1) * KX] = np.cos(angles)
        t[:, c, 1, g, j * KX : (j + 1) * KX] = np.sin(angles)
    return t.reshape(XC, 2, G * 128)


def twiddle_table():
    f, a = signed(KX), np.arange(GX)
    angles = ((f[None, :] * a[:, None] * XL) % NX) * (2.0 * math.pi / NX)
    t = np.zeros((GX, 8, G, 128), np.float32)
    for j in range(CG):
        t[:, 0, :, j * KX : (j + 1) * KX] = np.cos(angles)[:, None]
        t[:, 1, :, j * KX : (j + 1) * KX] = np.sin(angles)[:, None]
    return t.reshape(GX, 8, G * 128)


def group_tables():
    gather = np.zeros((CG, 128, 128), np.float32)
    spread = np.zeros((128, CG, 128), np.float32)
    eye = np.eye(KX, dtype=np.float32)
    for o in range(CG):
        for i in range(CG):
            gather[o, i * KX : (i + 1) * KX, o * KX : (o + 1) * KX] = eye
            spread[o * KX : (o + 1) * KX, o, i * KX : (i + 1) * KX] = eye
    return gather.reshape(CG * 128, 128), spread.reshape(128, CG * 128)


def mm(a, b):
    return jnp.dot(a, b, preferred_element_type=F32)


def split(v):
    high = v.astype(BF16)
    return high, (v - high.astype(F32)).astype(BF16)


def call(body, outs, *args, scratch=()):
    return pl.pallas_call(
        body,
        out_shape=outs,
        scratch_shapes=list(scratch),
        compiler_params=pltpu.CompilerParams(vmem_limit_bytes=56 * 2**20),
    )(*args)


def shape(*dims, dtype=F32):
    return jax.ShapeDtypeStruct(dims, dtype)


def pack_modes(c_ref, o_ref):
    for y in range(YL):
        blocks = []
        for t in range(2):
            v = c_ref[t, pl.ds(y, XC, stride=YL), :]
            vt = v.T
            for k in range(4 if t == 0 else 2):
                blocks.append(vt[k * GY : (k + 1) * GY])
        for part in range(2):
            row = jnp.concatenate(
                blocks[part * ML : (part + 1) * ML] + [jnp.zeros((GY, LT * 128 - ML * XC), F32)], axis=1
            )
            for lt in range(LT):
                o_ref[pl.ds(lt * 8 + part * YL + y, GY, stride=64), :] = row[:, lt * 128 : (lt + 1) * 128]


def unpack_modes(r_ref, g_ref):
    for y in range(YL):
        blocks = []
        for part in range(2):
            row = jnp.concatenate(
                [r_ref[pl.ds(lt * 8 + part * YL + y, GY, stride=64), :] for lt in range(LT)], axis=1
            )
            for m in range(ML):
                blocks.append(row[:, m * XC : (m + 1) * XC])
        top = jnp.concatenate(blocks[:4], axis=0)
        low = jnp.concatenate(blocks[4:] + [jnp.zeros((64, XC), F32)], axis=0)
        g_ref[0, pl.ds(y, XC, stride=YL), :] = top.T
        g_ref[1, pl.ds(y, XC, stride=YL), :] = low.T


def analyze_kernel(f_ref, t_ref, o_ref, c_ref):
    def body(i, _):
        v = jnp.concatenate([f_ref[i * 4 + k].reshape(C * YL, Q) for k in range(4)], axis=0)
        r = mm(v, t_ref[...])
        rows = pl.ds(pl.multiple_of(i * 320, 8), 320)
        c_ref[0, rows, :] = r[:, :128]
        c_ref[1, rows, :64] = r[:, 128:]
        return 0

    lax.fori_loop(0, 4, body, 0, unroll=True)
    pack_modes(c_ref, o_ref)


def forward_kernel(r_ref, f_ref, d_ref, w_ref, b_ref, s_ref, t_ref, out_ref, pre_ref, o_ref, g_ref, c_ref, sp_ref):
    unpack_modes(r_ref, g_ref)

    def body(i, _):
        rows = pl.ds(pl.multiple_of(i * 320, 8), 320)
        gh0, gl0 = split(g_ref[0, rows, :])
        gh1, gl1 = split(g_ref[1, rows, :])
        gh1, gl1 = gh1[:, :64], gl1[:, :64]
        lhs = jnp.concatenate([gh0, gh1, gl0, gl1, gh0, gh1], axis=1)
        sp_ref[...] = mm(lhs, s_ref[...])
        for k in range(2):
            x = i * 4 + 2 * k
            fv = jnp.concatenate([f_ref[x + h].reshape(C * YL, Q) for h in range(2)], axis=0)
            dv = jnp.concatenate([d_ref[x + h].reshape(C * YL, Q) for h in range(2)], axis=0)
            before = sp_ref[k * 160 : (k + 1) * 160, :] + mm(w_ref[...], fv) + b_ref[...]
            square = before * before
            tangent = jnp.tanh(before * (GELU_SCALE + (GELU_SCALE * GELU_CUBIC) * square))
            half = 0.5 + 0.5 * tangent
            result = before * half
            slope = half + result * (1.0 - tangent) * (GELU_SCALE + (3.0 * GELU_SCALE * GELU_CUBIC) * square)
            result = result.astype(BF16)
            pre = (dv.astype(F32) * slope).astype(BF16)
            for h in range(2):
                out_ref[x + h] = result[h * 80 : (h + 1) * 80].reshape(C, YL, Q)
            pre_ref[pl.ds(pl.multiple_of(x * 80, 16), 160), :] = pre
        r = mm(pre_ref[rows, :], t_ref[...])
        c_ref[0, rows, :] = r[:, :128]
        c_ref[1, rows, :64] = r[:, 128:]
        return 0

    lax.fori_loop(0, 4, body, 0)
    pack_modes(c_ref, o_ref)


def backward_kernel(r_ref, pre_ref, w_ref, s_ref, out_ref, g_ref, sp_ref):
    unpack_modes(r_ref, g_ref)

    def body(i, _):
        rows = pl.ds(pl.multiple_of(i * 320, 8), 320)
        gh0, gl0 = split(g_ref[0, rows, :])
        gh1, gl1 = split(g_ref[1, rows, :])
        gh1, gl1 = gh1[:, :64], gl1[:, :64]
        lhs = jnp.concatenate([gh0, gh1, gl0, gl1, gh0, gh1], axis=1)
        sp_ref[...] = mm(lhs, s_ref[...])
        for k in range(2):
            x = i * 4 + 2 * k
            pv = pre_ref[pl.ds(pl.multiple_of(x * 80, 16), 160), :]
            total = (sp_ref[k * 160 : (k + 1) * 160, :] + mm(w_ref[...], pv)).astype(BF16)
            for h in range(2):
                out_ref[x + h] = total[h * 80 : (h + 1) * 80].reshape(C, YL, Q)
        return 0

    lax.fori_loop(0, 4, body, 0)


def inward_kernel(r_ref, yh_ref, yl_ref, xh_ref, xl_ref, tw_ref, o_ref):
    tiles = []
    for lt in range(LT):
        v = r_ref[:, lt * 8 : (lt + 1) * 8, :].reshape(GY * 8, 128)
        vh, vl = split(v)
        tiles.append(mm(yh_ref[...], vh) + (mm(yh_ref[...], vl) + mm(yl_ref[...], vh)))
    row = jnp.concatenate(tiles, axis=1)
    y1 = jnp.concatenate([row[:, m * XC : (m + 1) * XC] for m in range(ML)], axis=0)
    vh, vl = split(y1)
    p = mm(vh, xh_ref[...]) + (mm(vl, xh_ref[...]) + mm(vh, xl_ref[...]))
    tc, ts = tw_ref[0:1, :], tw_ref[1:2, :]
    for m in range(ML):
        re, im = p[m * 48 : m * 48 + 24], p[m * 48 + 24 : m * 48 + 48]
        real = re[:, :512] + im[:, 512:]
        imag = im[:, :512] - re[:, 512:]
        parts = (real * tc + imag * ts, imag * tc - real * ts)
        for part in range(2):
            for ky in range(KYL):
                for g in range(G):
                    o_ref[pl.ds(g * 18 + part * 9 + ky * ML + m, GX, stride=ROWS), :] = parts[part][
                        ky * 8 : (ky + 1) * 8, g * 128 : (g + 1) * 128
                    ]


def outward_kernel(z_ref, xh_ref, xl_ref, y_ref, tw_ref, o_ref):
    tc, ts = tw_ref[0:1, :], tw_ref[1:2, :]
    rows = []
    for m in range(ML):
        parts = []
        for part in range(2):
            parts.append(
                jnp.concatenate(
                    [
                        jnp.concatenate(
                            [
                                z_ref[pl.ds(g * 18 + part * 9 + ky * ML + m, GX, stride=ROWS), :]
                                for g in range(G)
                            ],
                            axis=1,
                        )
                        for ky in range(KYL)
                    ],
                    axis=0,
                )
            )
        re, im = parts
        rows += [re * tc - im * ts, re * ts + im * tc]
    v = jnp.concatenate(rows, axis=0)
    vh, vl = split(v)
    p = mm(vh, xh_ref[...]) + (mm(vl, xh_ref[...]) + mm(vh, xl_ref[...]))
    tops, lows = [], []
    for m in range(ML):
        re, im = p[m * 48 : m * 48 + 24], p[m * 48 + 24 : m * 48 + 48]
        tops.append(re[:, :XC] - im[:, 384 : 384 + XC])
        lows.append(re[:, 384 : 384 + XC] + im[:, :XC])
    pad = [jnp.zeros((24, LT * 128 - ML * XC), F32)]
    v = jnp.concatenate([jnp.concatenate(tops + pad, axis=1), jnp.concatenate(lows + pad, axis=1)], axis=0)
    vh, vl = split(v)
    v3 = jnp.concatenate([vh, vl, vh], axis=0)
    for lt in range(LT):
        o = mm(y_ref[...], v3[:, lt * 128 : (lt + 1) * 128])
        o_ref[:, lt * 8 : (lt + 1) * 8, :] = o.reshape(GY, 8, 128)


def part_rows(ref, g, part):
    return ref[g * 18 + part * 9 : g * 18 + part * 9 + 9, :]


def send_all(o_ref, r_ref):
    for a in range(GX):
        o_ref[a] = r_ref[...]


def mix_kernel(q_ref, w_ref, e_ref, u_ref, o_ref, l_ref, r_ref):
    total = q_ref[0]
    for a in range(1, GX):
        total = total + q_ref[a]
    u_ref[...] = total
    us = [[part_rows(u_ref, g, part) for part in range(2)] for g in range(G)]
    l_ref[...] = jnp.zeros_like(l_ref)
    for o in range(C):
        real = imag = None
        for g in range(G):
            wr, wi = w_ref[o, g, 0], w_ref[o, g, 1]
            ur, ui = us[g]
            a, b = wr * ur - wi * ui, wr * ui + wi * ur
            real, imag = (a, b) if real is None else (real + a, imag + b)
        gi, oi = divmod(o, CG)
        l_ref[gi * 32 : gi * 32 + 9, oi * 128 : (oi + 1) * 128] = real
        l_ref[gi * 32 + 16 : gi * 32 + 25, oi * 128 : (oi + 1) * 128] = imag
    vh, vl = split(l_ref[...])
    v = (mm(vh, e_ref[...]) + mm(vl, e_ref[...])) * SCALE
    for g in range(G):
        for part in range(2):
            r_ref[g * 18 + part * 9 : g * 18 + part * 9 + 9, :] = v[g * 32 + part * 16 : g * 32 + part * 16 + 9]
    send_all(o_ref, r_ref)


def unmix_kernel(q_ref, w_ref, e_ref, s_ref, o_ref, l_ref, r_ref):
    total = q_ref[0]
    for a in range(1, GX):
        total = total + q_ref[a]
    r_ref[...] = total * SCALE
    l_ref[...] = jnp.zeros_like(l_ref)
    for g in range(G):
        for part in range(2):
            l_ref[g * 32 + part * 16 : g * 32 + part * 16 + 9, :] = part_rows(r_ref, g, part)
    vh, vl = split(l_ref[...])
    s_ref[...] = mm(vh, e_ref[...]) + mm(vl, e_ref[...])
    acc = [[None, None] for _ in range(G)]
    for o in range(C):
        gi, oi = divmod(o, CG)
        gr = s_ref[gi * 32 : gi * 32 + 9, oi * 128 : (oi + 1) * 128]
        gm = s_ref[gi * 32 + 16 : gi * 32 + 25, oi * 128 : (oi + 1) * 128]
        for g in range(G):
            wr, wi = w_ref[o, g, 0], w_ref[o, g, 1]
            a, b = wr * gr + wi * gm, wr * gm - wi * gr
            acc[g] = [a, b] if acc[g][0] is None else [acc[g][0] + a, acc[g][1] + b]
    for g in range(G):
        for part in range(2):
            r_ref[g * 18 + part * 9 : g * 18 + part * 9 + 9, :] = acc[g][part]
    send_all(o_ref, r_ref)


def outer_kernel(u_ref, s_ref, o_ref):
    us = [[part_rows(u_ref, g, part) for part in range(2)] for g in range(G)]
    for o in range(C):
        gi, oi = divmod(o, CG)
        gr = s_ref[gi * 32 : gi * 32 + 9, oi * 128 : (oi + 1) * 128]
        gm = s_ref[gi * 32 + 16 : gi * 32 + 25, oi * 128 : (oi + 1) * 128]
        for g in range(G):
            ur, ui = us[g]
            o_ref[o, g, 0] = gr * ur + gm * ui
            o_ref[o, g, 1] = gm * ur - gr * ui


def per_device(field, cotangent, spectral_weight, pointwise_weight, channel_bias):
    analysis, synthesis = zt_tables()
    toward = jnp.asarray(analysis.astype(jnp.bfloat16))
    toward_back = jnp.asarray(synthesis.astype(jnp.bfloat16))
    outward = jnp.asarray(three_rows(synthesis.T))
    outward_back = jnp.asarray(three_rows(analysis.T))
    ytab = y_table()
    y_in = [jnp.asarray(t) for t in halves(ytab)]
    yh, yl = halves(ytab.T)
    y_out = jnp.asarray(np.concatenate([yh, yh, yl], axis=1))
    xtab = x_table()
    x_in = [jnp.asarray(t) for t in halves(xtab.reshape(XC, 2 * G * 128))]
    xt = np.zeros((G * 128, 2, 384))
    xt[:, :, :XC] = np.transpose(xtab, (2, 1, 0))
    x_out = [jnp.asarray(t) for t in halves(xt.reshape(G * 128, 768))]
    gather, spread = group_tables()
    gather, spread = jnp.asarray(gather.astype(jnp.bfloat16)), jnp.asarray(spread.astype(jnp.bfloat16))
    twiddle = lax.dynamic_index_in_dim(jnp.asarray(twiddle_table()), lax.axis_index("gx"), 0, keepdims=False)

    f = jnp.transpose(field, (0, 2, 1, 3))
    d = jnp.transpose(cotangent, (0, 2, 1, 3))
    eye = jnp.eye(2, dtype=BF16)
    eye_y = jnp.eye(YL, dtype=BF16)
    mix_in = jnp.einsum("hk,io,yw->hoykiw", eye, pointwise_weight, eye_y).reshape(160, 160)
    mix_back = jnp.einsum("hk,io,yw->hiykow", eye, pointwise_weight, eye_y).reshape(160, 160)
    bias = jnp.broadcast_to(channel_bias[None, :, None], (2, C, YL)).reshape(160, 1)
    w = spectral_weight.reshape(2, G, CG, C, KX, KYL, ML)
    w = jnp.transpose(w, (3, 1, 0, 5, 6, 2, 4)).reshape(C, G, 2, MODES, KC)
    w = jnp.pad(w, ((0, 0),) * 4 + ((0, 128 - KC),))

    def over_y(v):
        return lax.all_to_all(v.reshape(GY, 64, 128), "gy", split_axis=0, concat_axis=0, tiled=True)

    def over_x(v):
        return lax.all_to_all(v.reshape(GX, ROWS, 128), "gx", split_axis=0, concat_axis=0, tiled=True)

    def inward(v):
        return over_x(call(inward_kernel, shape(GX * ROWS, 128), over_y(v), *y_in, *x_in, twiddle))

    def spread_out(v):
        v = over_x(v).reshape(GX * ROWS, 128)
        v = call(outward_kernel, shape(GY, 64, 128), v, *x_out, y_out, twiddle)
        return over_y(v).reshape(GY * 64, 128)

    cells = pltpu.VMEM((2, CELLS, 128), F32)
    part = pltpu.VMEM((320, Q), F32)
    rows = pltpu.VMEM((ROWS, 128), F32)
    v = call(analyze_kernel, shape(GY * 64, 128), f, toward, scratch=[cells])
    v = inward(v)
    u, v = call(
        mix_kernel, (shape(ROWS, 128), shape(GX, ROWS, 128)), v, w, gather,
        scratch=[pltpu.VMEM((128, CG * 128), F32), rows],
    )
    v = spread_out(v)
    output, pre, v = call(
        forward_kernel,
        (shape(XL, C, YL, Q, dtype=BF16), shape(CELLS, Q, dtype=BF16), shape(GY * 64, 128)),
        v, f, d, mix_in, bias, outward, toward_back,
        scratch=[cells, cells, part],
    )
    v = inward(v)
    s, v = call(
        unmix_kernel, (shape(128, CG * 128), shape(GX, ROWS, 128)), v, w, spread,
        scratch=[pltpu.VMEM((128, 128), F32), rows],
    )
    gw = call(outer_kernel, shape(C, G, 2, MODES, 128), u, s)
    gw = gw[..., :KC].reshape(C, G, 2, KYL, ML, CG, KX)
    grad_weight = jnp.transpose(gw, (2, 1, 5, 0, 6, 3, 4)).reshape(2, C, C, KX, KYL, ML)
    v = spread_out(v)
    grad_field = call(
        backward_kernel, shape(XL, C, YL, Q, dtype=BF16), v, pre, mix_back, outward_back,
        scratch=[cells, part],
    )
    return (jnp.transpose(output, (0, 2, 1, 3)), jnp.transpose(grad_field, (0, 2, 1, 3)), grad_weight)


def solution(mesh):
    grid = P("gx", "gy", None, None)
    modes = P(None, None, None, None, "gx", "gy")
    return jax.shard_map(
        per_device,
        mesh=mesh,
        in_specs=(grid, grid, modes, P(), P()),
        out_specs=(grid, grid, modes),
        check_vma=False,
    )
```

```python
import math

import jax
import jax.numpy as jnp
import numpy as np
from jax import lax
from jax.experimental import pallas as pl
from jax.experimental.pallas import tpu as pltpu
from jax.sharding import PartitionSpec as P

NX = 128
NY = 128
NZ = 64
NT = 16
C = 20
KX = 24
KY = 24
KZ = 12
KT = 8

GX = 8
GY = 32
XL = NX // GX
YL = NY // GY
KYL = KY // GX
ML = KZ * KT // GY
XC = XL * C
CELLS = XL * C * YL
Q = NZ * NT
N = 2 * ML * GY
LT = 7
CHUNK = 60
G = 4
CG = C // G
KC = CG * KX
MODES = KYL * ML
ROWS = G * 2 * MODES

GELU_SCALE = math.sqrt(2.0 / math.pi)
GELU_CUBIC = 0.044715
F32 = jnp.float32
BF16 = jnp.bfloat16
SCALE = 1.0 / (NX * NY)


def signed(count):
    j = np.arange(count)
    return np.where(j < count // 2, j, j - count)


def halves(table):
    table = np.asarray(table, np.float32)
    high = table.astype(jnp.bfloat16)
    low = (table - high.astype(np.float32)).astype(jnp.bfloat16)
    return high, low


def zt_tables():
    q = np.arange(Q)
    m = (np.arange(GY)[None, :] * ML + np.arange(ML)[:, None]).reshape(-1)
    fz, kt = signed(KZ)[m // KT], m % KT
    phase = (fz[None, :] * (q // NT)[:, None] * NT + kt[None, :] * (q % NT)[:, None] * NZ) % Q
    angles = phase * (2.0 * math.pi / Q)
    weights = np.where(kt == 0, 1.0, 2.0) / Q
    analysis = np.concatenate([np.cos(angles), -np.sin(angles)], axis=1)
    synthesis = analysis * np.concatenate([weights, weights])[None, :]
    return analysis.astype(np.float32), synthesis.astype(np.float32)


def three_rows(table):
    high, low = halves(table)
    return np.concatenate([high, high, low], axis=0)


def y_table():
    ky = (np.arange(GX)[None, :] * KYL + np.arange(KYL)[:, None]).reshape(-1)
    f = signed(KY)[ky]
    n = np.arange(NY)
    angles = ((f[:, None] * n[None, :]) % NY) * (2.0 * math.pi / NY)
    c, s = np.cos(angles), np.sin(angles)
    t = np.zeros((2, KY, GY, 2, YL))
    c4, s4 = c.reshape(KY, GY, YL), s.reshape(KY, GY, YL)
    t[0, :, :, 0], t[0, :, :, 1] = c4, s4
    t[1, :, :, 0], t[1, :, :, 1] = -s4, c4
    return np.transpose(t, (0, 1, 3, 4, 2)).reshape(2 * KY, 2 * YL * GY)


def x_table():
    f, x = signed(KX), np.arange(XL)
    angles = ((f[None, :] * x[:, None]) % NX) * (2.0 * math.pi / NX)
    t = np.zeros((XL, C, 2, G, 128))
    for c in range(C):
        g, j = divmod(c, CG)
        t[:, c, 0, g, j * KX : (j + 1) * KX] = np.cos(angles)
        t[:, c, 1, g, j * KX : (j + 1) * KX] = np.sin(angles)
    return t.reshape(XC, 2, G * 128)


def twiddle_table():
    f, a = signed(KX), np.arange(GX)
    angles = ((f[None, :] * a[:, None] * XL) % NX) * (2.0 * math.pi / NX)
    t = np.zeros((GX, 8, G, 128), np.float32)
    for j in range(CG):
        t[:, 0, :, j * KX : (j + 1) * KX] = np.cos(angles)[:, None]
        t[:, 1, :, j * KX : (j + 1) * KX] = np.sin(angles)[:, None]
    return t.reshape(GX, 8, G * 128)


def group_tables():
    gather = np.zeros((CG, 128, 128), np.float32)
    spread = np.zeros((128, CG, 128), np.float32)
    eye = np.eye(KX, dtype=np.float32)
    for o in range(CG):
        for i in range(CG):
            gather[o, i * KX : (i + 1) * KX, o * KX : (o + 1) * KX] = eye
            spread[o * KX : (o + 1) * KX, o, i * KX : (i + 1) * KX] = eye
    return gather.reshape(CG * 128, 128), spread.reshape(128, CG * 128)


def mm(a, b):
    return jnp.dot(a, b, preferred_element_type=F32)


def split(v):
    high = v.astype(BF16)
    return high, (v - high.astype(F32)).astype(BF16)


def call(body, outs, *args, scratch=(), mib=12):
    return pl.pallas_call(
        body,
        out_shape=outs,
        scratch_shapes=list(scratch),
        compiler_params=pltpu.CompilerParams(vmem_limit_bytes=mib * 2**20),
    )(*args)


def shape(*dims, dtype=F32):
    return jax.ShapeDtypeStruct(dims, dtype)


def held(*dims, dtype=F32):
    return pltpu.VMEM(dims, dtype)


def pin(*values):
    return [pltpu.with_memory_space_constraint(v, pltpu.VMEM) for v in values]


def far(*values):
    return [pltpu.with_memory_space_constraint(v, pltpu.HBM) for v in values]


def fetch_kernel(*refs):
    count = len(refs) // 2
    sems = refs[-1]
    copies = [pltpu.make_async_copy(refs[i], refs[count + i], sems.at[i]) for i in range(count)]
    for copy in copies:
        copy.start()
    for copy in copies:
        copy.wait()


def fetch(*arrays):
    return pl.pallas_call(
        fetch_kernel,
        out_shape=tuple(held(*a.shape, dtype=a.dtype) for a in arrays),
        in_specs=[pl.BlockSpec(memory_space=pltpu.HBM)] * len(arrays),
        scratch_shapes=[pltpu.SemaphoreType.DMA((len(arrays),))],
        compiler_params=pltpu.CompilerParams(vmem_limit_bytes=2**20),
    )(*far(*arrays))


def pack_modes(c_ref, o_ref):
    for y in range(YL):
        blocks = []
        for t in range(2):
            v = c_ref[t, pl.ds(y, XC, stride=YL), :]
            vt = v.T
            for k in range(4 if t == 0 else 2):
                blocks.append(vt[k * GY : (k + 1) * GY])
        rows = [jnp.concatenate(blocks[part * ML : (part + 1) * ML], axis=1) for part in range(2)]
        for part in range(2):
            for lt in range(LT):
                o_ref[pl.ds(lt * 8 + part * YL + y, GY, stride=CHUNK), :] = rows[part][:, lt * 128 : (lt + 1) * 128]
        o_ref[pl.ds(LT * 8 + y, GY, stride=CHUNK), :] = jnp.concatenate([r[:, LT * 128 :] for r in rows], axis=1)


def unpack_modes(r_ref, g_ref):
    for y in range(YL):
        blocks = []
        last = r_ref[pl.ds(LT * 8 + y, GY, stride=CHUNK), :]
        for part in range(2):
            row = jnp.concatenate(
                [r_ref[pl.ds(lt * 8 + part * YL + y, GY, stride=CHUNK), :] for lt in range(LT)]
                + [last[:, part * 64 : part * 64 + 64]],
                axis=1,
            )
            for m in range(ML):
                blocks.append(row[:, m * XC : (m + 1) * XC])
        top = jnp.concatenate(blocks[:4], axis=0)
        low = jnp.concatenate(blocks[4:] + [jnp.zeros((64, XC), F32)], axis=0)
        g_ref[0, pl.ds(y, XC, stride=YL), :] = top.T
        g_ref[1, pl.ds(y, XC, stride=YL), :] = low.T


def analyze_kernel(f_ref, table_ref, o_ref, c_ref, v_ref, t_ref, sems):
    table = pltpu.make_async_copy(table_ref, t_ref, sems.at[4])
    table.start()
    copies = [pltpu.make_async_copy(f_ref.at[pl.ds(i * 4, 4)], v_ref.at[pl.ds(i * 4, 4)], sems.at[i]) for i in range(4)]
    for copy in copies:
        copy.start()
    table.wait()
    for i in range(4):
        copies[i].wait()
        v = jnp.concatenate([v_ref[i * 4 + k].reshape(C * YL, Q) for k in range(4)], axis=0)
        r = mm(v, t_ref[...])
        c_ref[0, i * 320 : (i + 1) * 320, :] = r[:, :128]
        c_ref[1, i * 320 : (i + 1) * 320, :64] = r[:, 128:]
    pack_modes(c_ref, o_ref)


def widen(table, e_ref, et_ref, mask_ref):
    tall = mm(e_ref[...], table).astype(BF16)
    return mm(tall, et_ref[...]).astype(BF16) * mask_ref[...]


def linear_kernel(f_ref, d_ref, w_ref, b_ref, e_ref, et_ref, mask_ref, lin_ref, row_ref):
    mix = widen(w_ref[...], e_ref, et_ref, mask_ref)
    bias = jnp.sum(e_ref[...].astype(F32) * b_ref[...], axis=1, keepdims=True)

    def body(i, _):
        x = 2 * i
        rows = pl.ds(pl.multiple_of(i * 160, 16), 160)
        fv = jnp.concatenate([f_ref[x + h].reshape(C * YL, Q) for h in range(2)], axis=0)
        lin_ref[rows, :] = mm(mix, fv) + bias
        row_ref[rows, :] = jnp.concatenate([d_ref[x + h].reshape(C * YL, Q) for h in range(2)], axis=0)
        return 0

    lax.fori_loop(0, XL // 2, body, 0)


def linear_back_kernel(p_ref, w_ref, e_ref, et_ref, mask_ref, lin_ref):
    mix = widen(w_ref[...], e_ref, et_ref, mask_ref)

    def body(i, _):
        rows = pl.ds(pl.multiple_of(i * 160, 16), 160)
        lin_ref[rows, :] = mm(mix, p_ref[rows, :])
        return 0

    lax.fori_loop(0, XL // 2, body, 0)


def synthesis_rows(g_ref, rows):
    gh0, gl0 = split(g_ref[0, rows, :])
    gh1, gl1 = split(g_ref[1, rows, :])
    gh1, gl1 = gh1[:, :64], gl1[:, :64]
    return jnp.concatenate([gh0, gh1, gl0, gl1, gh0, gh1], axis=1)


def pieces(source, target, sems):
    return [
        pltpu.make_async_copy(source.at[pl.ds(i * n, n)], target.at[pl.ds(i * n, n)], sems.at[i])
        for n in [source.shape[0] // 4]
        for i in range(4)
    ]


def forward_kernel(
    r_ref, lin_hbm, d_hbm, s_ref, t_hbm, out_hbm, pre_hbm, o_ref,
    g_ref, c_ref, lin_ref, d_ref, sp_ref, t_ref, out_ref, pre_ref, sems, sem,
):
    table = pltpu.make_async_copy(t_hbm, t_ref, sem)
    lin_in, d_in = pieces(lin_hbm, lin_ref, sems.at[0]), pieces(d_hbm, d_ref, sems.at[1])
    out_out, pre_out = pieces(out_ref, out_hbm, sems.at[2]), pieces(pre_ref, pre_hbm, sems.at[3])
    for i in range(4):
        lin_in[i].start()
        d_in[i].start()
        if i == 0:
            table.start()
    unpack_modes(r_ref, g_ref)
    table.wait()
    for i in range(4):
        rows = slice(i * 320, (i + 1) * 320)
        sp_ref[...] = mm(synthesis_rows(g_ref, rows), s_ref[...])
        lin_in[i].wait()
        d_in[i].wait()

        def body(k, _, i=i):
            at = pl.ds(pl.multiple_of(i * 320 + k * 80, 16), 80)
            before = sp_ref[pl.ds(pl.multiple_of(k * 80, 16), 80), :] + lin_ref[at, :]
            square = before * before
            tangent = jnp.tanh(before * (GELU_SCALE + (GELU_SCALE * GELU_CUBIC) * square))
            half = 0.5 + 0.5 * tangent
            result = before * half
            slope = half + result * (1.0 - tangent) * (GELU_SCALE + (3.0 * GELU_SCALE * GELU_CUBIC) * square)
            pre_ref[at, :] = (d_ref[at, :].astype(F32) * slope).astype(BF16)
            out_ref[i * 4 + k] = result.astype(BF16).reshape(C, YL, Q)
            return 0

        lax.fori_loop(0, 4, body, 0)
        out_out[i].start()
        pre_out[i].start()
        r = mm(pre_ref[rows, :], t_ref[...])
        c_ref[0, rows, :] = r[:, :128]
        c_ref[1, rows, :64] = r[:, 128:]
    pack_modes(c_ref, o_ref)
    for i in range(4):
        out_out[i].wait()
        pre_out[i].wait()


def backward_kernel(r_ref, lin_hbm, s_ref, out_hbm, g_ref, sp_ref, lin_ref, out_ref, sems):
    lin_in, out_out = pieces(lin_hbm, lin_ref, sems.at[0]), pieces(out_ref, out_hbm, sems.at[1])
    for i in range(4):
        lin_in[i].start()
    unpack_modes(r_ref, g_ref)
    for i in range(4):
        rows = slice(i * 320, (i + 1) * 320)
        sp_ref[...] = mm(synthesis_rows(g_ref, rows), s_ref[...])
        lin_in[i].wait()
        for k in range(4):
            total = sp_ref[k * 80 : (k + 1) * 80, :] + lin_ref[i * 320 + k * 80 : i * 320 + (k + 1) * 80, :]
            out_ref[i * 4 + k] = total.astype(BF16).reshape(C, YL, Q)
        out_out[i].start()
    for i in range(4):
        out_out[i].wait()


def inward_kernel(r_ref, yh_ref, yl_ref, xh_ref, xl_ref, tw_ref, o_ref, copy=None):
    columns = []
    for lt in range(LT):
        columns.append([r_ref[pl.ds(lt * 8 + k, GY, stride=CHUNK), :] for k in range(8)])
    last = [r_ref[pl.ds(LT * 8 + k, GY, stride=CHUNK), :] for k in range(YL)]
    columns.append([v[:, :64] for v in last] + [v[:, 64:] for v in last])
    tiles = []
    for column in columns:
        vh, vl = split(jnp.concatenate(column, axis=0))
        tiles.append(mm(yh_ref[...], vh) + (mm(yh_ref[...], vl) + mm(yl_ref[...], vh)))
    row = jnp.concatenate(tiles, axis=1)
    y1 = jnp.concatenate([row[:, m * XC : (m + 1) * XC] for m in range(ML)], axis=0)
    vh, vl = split(y1)
    if copy is not None:
        copy.wait()
    p = mm(vh, xh_ref[...]) + (mm(vl, xh_ref[...]) + mm(vh, xl_ref[...]))
    tc, ts = tw_ref[0:1, :], tw_ref[1:2, :]
    for m in range(ML):
        re, im = p[m * 48 : m * 48 + 24], p[m * 48 + 24 : m * 48 + 48]
        real = re[:, :512] + im[:, 512:]
        imag = im[:, :512] - re[:, 512:]
        parts = (real * tc + imag * ts, imag * tc - real * ts)
        for part in range(2):
            for ky in range(KYL):
                for g in range(G):
                    o_ref[pl.ds(g * 18 + part * 9 + ky * ML + m, GX, stride=ROWS), :] = parts[part][
                        ky * 8 : (ky + 1) * 8, g * 128 : (g + 1) * 128
                    ]


def first_inward_kernel(r_ref, yh_ref, yl_ref, xh_ref, xl_hbm, tw_ref, o_ref, xl_ref, sem):
    copy = pltpu.make_async_copy(xl_hbm, xl_ref, sem)
    copy.start()
    inward_kernel(r_ref, yh_ref, yl_ref, xh_ref, xl_ref, tw_ref, o_ref, copy)


def outward_kernel(z_ref, xh_ref, xl_ref, y_ref, tw_ref, o_ref):
    tc, ts = tw_ref[0:1, :], tw_ref[1:2, :]
    rows = []
    for m in range(ML):
        parts = []
        for part in range(2):
            parts.append(
                jnp.concatenate(
                    [
                        jnp.concatenate(
                            [
                                z_ref[pl.ds(g * 18 + part * 9 + ky * ML + m, GX, stride=ROWS), :]
                                for g in range(G)
                            ],
                            axis=1,
                        )
                        for ky in range(KYL)
                    ],
                    axis=0,
                )
            )
        re, im = parts
        rows += [re * tc - im * ts, re * ts + im * tc]
    v = jnp.concatenate(rows, axis=0)
    vh, vl = split(v)
    p = mm(vh, xh_ref[...]) + (mm(vl, xh_ref[...]) + mm(vh, xl_ref[...]))
    tops, lows = [], []
    for m in range(ML):
        re, im = p[m * 48 : m * 48 + 24], p[m * 48 + 24 : m * 48 + 48]
        tops.append(re[:, :XC] - im[:, 384 : 384 + XC])
        lows.append(re[:, 384 : 384 + XC] + im[:, :XC])
    v = jnp.concatenate([jnp.concatenate(tops, axis=1), jnp.concatenate(lows, axis=1)], axis=0)
    vh, vl = split(v)
    v3 = jnp.concatenate([vh, vl, vh], axis=0)
    for lt in range(LT):
        o = mm(y_ref[...], v3[:, lt * 128 : (lt + 1) * 128])
        for k in range(8):
            o_ref[pl.ds(lt * 8 + k, GY, stride=CHUNK), :] = o[k * GY : (k + 1) * GY]
    o = mm(y_ref[...], v3[:, LT * 128 :])
    for k in range(YL):
        o_ref[pl.ds(LT * 8 + k, GY, stride=CHUNK), :] = jnp.concatenate(
            [o[k * GY : (k + 1) * GY], o[(YL + k) * GY : (YL + k + 1) * GY]], axis=1
        )


def part_rows(ref, g, part):
    return ref[g * 18 + part * 9 : g * 18 + part * 9 + 9, :]


def send_all(o_ref, r_ref):
    for a in range(GX):
        o_ref[a] = r_ref[...]


def mix_kernel(q_ref, w_ref, e_ref, u_ref, o_ref, l_ref, r_ref):
    total = q_ref[0]
    for a in range(1, GX):
        total = total + q_ref[a]
    u_ref[...] = total
    us = [[part_rows(u_ref, g, part) for part in range(2)] for g in range(G)]
    l_ref[...] = jnp.zeros_like(l_ref)
    for o in range(C):
        real = imag = None
        for g in range(G):
            wr, wi = w_ref[o, g, 0], w_ref[o, g, 1]
            ur, ui = us[g]
            a, b = wr * ur - wi * ui, wr * ui + wi * ur
            real, imag = (a, b) if real is None else (real + a, imag + b)
        gi, oi = divmod(o, CG)
        l_ref[gi * 32 : gi * 32 + 9, oi * 128 : (oi + 1) * 128] = real
        l_ref[gi * 32 + 16 : gi * 32 + 25, oi * 128 : (oi + 1) * 128] = imag
    vh, vl = split(l_ref[...])
    v = (mm(vh, e_ref[...]) + mm(vl, e_ref[...])) * SCALE
    for g in range(G):
        for part in range(2):
            r_ref[g * 18 + part * 9 : g * 18 + part * 9 + 9, :] = v[g * 32 + part * 16 : g * 32 + part * 16 + 9]
    send_all(o_ref, r_ref)


def unmix_kernel(q_ref, w_ref, e_ref, s_ref, o_ref, l_ref, r_ref):
    total = q_ref[0]
    for a in range(1, GX):
        total = total + q_ref[a]
    r_ref[...] = total * SCALE
    l_ref[...] = jnp.zeros_like(l_ref)
    for g in range(G):
        for part in range(2):
            l_ref[g * 32 + part * 16 : g * 32 + part * 16 + 9, :] = part_rows(r_ref, g, part)
    vh, vl = split(l_ref[...])
    s_ref[...] = mm(vh, e_ref[...]) + mm(vl, e_ref[...])
    acc = [[None, None] for _ in range(G)]
    for o in range(C):
        gi, oi = divmod(o, CG)
        gr = s_ref[gi * 32 : gi * 32 + 9, oi * 128 : (oi + 1) * 128]
        gm = s_ref[gi * 32 + 16 : gi * 32 + 25, oi * 128 : (oi + 1) * 128]
        for g in range(G):
            wr, wi = w_ref[o, g, 0], w_ref[o, g, 1]
            a, b = wr * gr + wi * gm, wr * gm - wi * gr
            acc[g] = [a, b] if acc[g][0] is None else [acc[g][0] + a, acc[g][1] + b]
    for g in range(G):
        for part in range(2):
            r_ref[g * 18 + part * 9 : g * 18 + part * 9 + 9, :] = acc[g][part]
    send_all(o_ref, r_ref)


def outer_kernel(u_ref, s_ref, o_ref):
    us = [[part_rows(u_ref, g, part) for part in range(2)] for g in range(G)]
    for o in range(C):
        gi, oi = divmod(o, CG)
        gr = s_ref[gi * 32 : gi * 32 + 9, oi * 128 : (oi + 1) * 128]
        gm = s_ref[gi * 32 + 16 : gi * 32 + 25, oi * 128 : (oi + 1) * 128]
        for g in range(G):
            ur, ui = us[g]
            o_ref[o, g, 0] = gr * ur + gm * ui
            o_ref[o, g, 1] = gm * ur - gr * ui


def per_device(field, cotangent, spectral_weight, pointwise_weight, channel_bias):
    analysis, synthesis = zt_tables()
    toward = jnp.asarray(analysis.astype(jnp.bfloat16))
    toward_back = jnp.asarray(synthesis.astype(jnp.bfloat16))
    outward = jnp.asarray(three_rows(synthesis.T))
    outward_back = jnp.asarray(three_rows(analysis.T))
    ytab = y_table()
    y_in = [jnp.asarray(t) for t in halves(ytab)]
    yh, yl = halves(ytab.T)
    y_out = jnp.asarray(np.concatenate([yh, yh, yl], axis=1))
    xtab = x_table()
    x_in = [jnp.asarray(t) for t in halves(xtab.reshape(XC, 2 * G * 128))]
    xt = np.zeros((G * 128, 2, 384))
    xt[:, :, :XC] = np.transpose(xtab, (2, 1, 0))
    x_out = [jnp.asarray(t) for t in halves(xt.reshape(G * 128, 768))]
    gather, spread = group_tables()
    gather, spread = jnp.asarray(gather.astype(jnp.bfloat16)), jnp.asarray(spread.astype(jnp.bfloat16))
    twiddle = lax.dynamic_index_in_dim(jnp.asarray(twiddle_table()), lax.axis_index("gx"), 0, keepdims=False)

    f = jnp.transpose(field, (0, 2, 1, 3))
    d = jnp.transpose(cotangent, (0, 2, 1, 3))
    row_channel = (np.arange(160) // YL) % C
    pick = (row_channel[:, None] == np.arange(C)[None, :]).astype(jnp.bfloat16)
    cell = (np.arange(160) // (C * YL)) * YL + np.arange(160) % YL
    wide = [jnp.asarray(v) for v in (pick, pick.T, (cell[:, None] == cell[None, :]).astype(jnp.bfloat16))]
    w = spectral_weight.reshape(2, G, CG, C, KX, KYL, ML)
    w = jnp.transpose(w, (3, 1, 0, 5, 6, 2, 4)).reshape(C, G, 2, MODES, KC)
    w = jnp.pad(w, ((0, 0),) * 4 + ((0, 128 - KC),))

    hbm, vmem = pl.BlockSpec(memory_space=pltpu.HBM), pl.BlockSpec(memory_space=pltpu.VMEM)

    def over_y(v):
        return lax.all_to_all(v.reshape(GY, 1, CHUNK * 128), "gy", split_axis=0, concat_axis=0, tiled=True).reshape(
            GY * CHUNK, 128
        )

    def over_x(v):
        return lax.all_to_all(v.reshape(GX, ROWS, 128), "gx", split_axis=0, concat_axis=0, tiled=True)

    def outward_part(v):
        return call(outward_kernel, shape(GY * CHUNK, 128), over_x(v).reshape(GX * ROWS, 128), *x_out, y_out, twiddle)

    cells = pltpu.VMEM((2, CELLS, 128), F32)
    rows = pltpu.VMEM((ROWS, 128), F32)
    full, full16 = pltpu.VMEM((CELLS, Q), F32), pltpu.VMEM((CELLS, Q), BF16)
    native = pltpu.VMEM((XL, C, YL, Q), BF16)
    grid, grid16 = pltpu.HBM((CELLS, Q), F32), pltpu.HBM((CELLS, Q), BF16)
    v = pl.pallas_call(
        analyze_kernel,
        out_shape=shape(GY * CHUNK, 128),
        in_specs=[hbm] * 2,
        scratch_shapes=[cells, native, pltpu.VMEM((Q, N), BF16), pltpu.SemaphoreType.DMA((5,))],
        compiler_params=pltpu.CompilerParams(vmem_limit_bytes=12 * 2**20),
    )(*far(f, toward))
    v, tables = lax.optimization_barrier((v, (*y_in, x_in[0], gather)))
    v, w, (*inner, gather) = lax.optimization_barrier((over_y(v), w, fetch(*tables)))
    v = pl.pallas_call(
        first_inward_kernel,
        out_shape=shape(GX * ROWS, 128),
        in_specs=[vmem] * 4 + [hbm, vmem],
        scratch_shapes=[pltpu.VMEM((XC, 2 * G * 128), BF16), pltpu.SemaphoreType.DMA(())],
        compiler_params=pltpu.CompilerParams(vmem_limit_bytes=12 * 2**20),
    )(v, *pin(*inner), *far(x_in[1]), twiddle)
    u, v = call(
        mix_kernel, (shape(ROWS, 128), shape(GX, ROWS, 128)), over_x(v), w, *pin(gather),
        scratch=[pltpu.VMEM((128, CG * 128), F32), rows],
    )
    v, f, d, table = lax.optimization_barrier((outward_part(v), f, d, outward))
    lin, d = call(
        linear_kernel, (grid, grid16), f, d, pointwise_weight.T, channel_bias.reshape(1, C), *wide, mib=18
    )
    v, lin, d, (table,) = lax.optimization_barrier((over_y(v), lin, d, fetch(table)))
    output, pre, v = pl.pallas_call(
        forward_kernel,
        out_shape=(shape(XL, C, YL, Q, dtype=BF16), grid16, shape(GY * CHUNK, 128)),
        in_specs=[vmem, hbm, hbm, vmem, hbm],
        out_specs=(hbm, hbm, vmem),
        scratch_shapes=[
            cells, cells, full, full16, pltpu.VMEM((320, Q), F32), pltpu.VMEM((Q, N), BF16), native, full16,
            pltpu.SemaphoreType.DMA((4, 4)), pltpu.SemaphoreType.DMA(()),
        ],
        compiler_params=pltpu.CompilerParams(vmem_limit_bytes=28 * 2**20),
    )(v, *far(lin, d), *pin(table), *far(toward_back))
    v = call(inward_kernel, shape(GX * ROWS, 128), over_y(v), *y_in, *x_in, twiddle)
    v = over_x(v)
    s, v = call(
        unmix_kernel, (shape(128, CG * 128), shape(GX, ROWS, 128)), v, w, spread,
        scratch=[pltpu.VMEM((128, 128), F32), rows],
    )
    v, s, pre, table = lax.optimization_barrier((outward_part(v), s, pre, outward_back))
    lin = call(linear_back_kernel, grid, pre, pointwise_weight, *wide, mib=14)
    gw = call(outer_kernel, shape(C, G, 2, MODES, 128), u, s)
    gw = gw[..., :KC].reshape(C, G, 2, KYL, ML, CG, KX)
    grad_weight = jnp.transpose(gw, (2, 1, 5, 0, 6, 3, 4)).reshape(2, C, C, KX, KYL, ML)
    v, lin, (table,) = lax.optimization_barrier((over_y(v), lin, fetch(table)))
    grad_field = pl.pallas_call(
        backward_kernel,
        out_shape=shape(XL, C, YL, Q, dtype=BF16),
        in_specs=[vmem, hbm, vmem],
        out_specs=hbm,
        scratch_shapes=[cells, pltpu.VMEM((320, Q), F32), full, native, pltpu.SemaphoreType.DMA((2, 4))],
        compiler_params=pltpu.CompilerParams(vmem_limit_bytes=18 * 2**20),
    )(v, *far(lin), *pin(table))
    return (jnp.transpose(output, (0, 2, 1, 3)), jnp.transpose(grad_field, (0, 2, 1, 3)), grad_weight)


def solution(mesh):
    grid = P("gx", "gy", None, None)
    modes = P(None, None, None, None, "gx", "gy")
    return jax.shard_map(
        per_device,
        mesh=mesh,
        in_specs=(grid, grid, modes, P(), P()),
        out_specs=(grid, grid, modes),
        check_vma=False,
    )
```

```python
import math

import jax
import jax.numpy as jnp
import numpy as np
from jax import lax
from jax.experimental import pallas as pl
from jax.experimental.pallas import tpu as pltpu
from jax.sharding import PartitionSpec as P

NX = 128
NY = 128
NZ = 64
NT = 16
C = 20
KX = 24
KY = 24
KZ = 12
KT = 8

GX = 8
GY = 32
XL = NX // GX
YL = NY // GY
KYL = KY // GX
ML = KZ * KT // GY
XC = XL * C
CELLS = XL * C * YL
Q = NZ * NT
N = 2 * ML * GY
HALF = C // 2
HC = XL * HALF
KEEP = HC * YL
SWAP = KEEP * 3 // 2
LT = 6
CHUNK = LT * 8
G = 4
CG = C // G
KC = CG * KX
MODES = KYL * ML
ROWS = G * 2 * MODES
XROWS = ROWS // 2

GELU_SCALE = math.sqrt(2.0 / math.pi)
GELU_CUBIC = 0.044715
F32 = jnp.float32
BF16 = jnp.bfloat16
SCALE = 1.0 / (NX * NY)


def signed(count):
    j = np.arange(count)
    return np.where(j < count // 2, j, j - count)


def halves(table):
    table = np.asarray(table, np.float32)
    high = table.astype(jnp.bfloat16)
    low = (table - high.astype(np.float32)).astype(jnp.bfloat16)
    return high, low


def zt_tables():
    q = np.arange(Q)
    m = (np.arange(GY)[None, :] * ML + np.arange(ML)[:, None]).reshape(-1)
    fz, kt = signed(KZ)[m // KT], m % KT
    phase = (fz[None, :] * (q // NT)[:, None] * NT + kt[None, :] * (q % NT)[:, None] * NZ) % Q
    angles = phase * (2.0 * math.pi / Q)
    weights = np.where(kt == 0, 1.0, 2.0) / Q
    analysis = np.concatenate([np.cos(angles), -np.sin(angles)], axis=1)
    synthesis = analysis * np.concatenate([weights, weights])[None, :]
    return analysis.astype(np.float32), synthesis.astype(np.float32)


def three_rows(table):
    high, low = halves(table)
    return np.concatenate([high, high, low], axis=0)


def y_table():
    ky = (np.arange(GX)[None, :] * KYL + np.arange(KYL)[:, None]).reshape(-1)
    f = signed(KY)[ky]
    n = np.arange(NY)
    angles = ((f[:, None] * n[None, :]) % NY) * (2.0 * math.pi / NY)
    c, s = np.cos(angles), np.sin(angles)
    t = np.zeros((2, KY, GY, 2, YL))
    c4, s4 = c.reshape(KY, GY, YL), s.reshape(KY, GY, YL)
    t[0, :, :, 0], t[0, :, :, 1] = c4, s4
    t[1, :, :, 0], t[1, :, :, 1] = -s4, c4
    return np.transpose(t, (0, 1, 3, 4, 2)).reshape(2 * KY, 2 * YL * GY)


def x_tables():
    f = signed(KX)
    t = np.zeros((GX, 2, XL, HALF, 2, 2, 128))
    for a in range(GX):
        for side in range(2):
            cells = XL * (a ^ side) + np.arange(XL)
            angles = ((f[None, :] * cells[:, None]) % NX) * (2.0 * math.pi / NX)
            for c in range(HALF):
                g, j = divmod(c, CG)
                t[a, side, :, c, 0, g, j * KX : (j + 1) * KX] = np.cos(angles)
                t[a, side, :, c, 1, g, j * KX : (j + 1) * KX] = np.sin(angles)
    turned = np.zeros((GX, 256, 2, 384))
    turned[..., :XC] = np.transpose(t, (0, 5, 6, 4, 1, 2, 3)).reshape(GX, 256, 2, XC)
    return t.reshape(GX, XC, 512), turned.reshape(GX, 256, 768)


def group_tables():
    gather = np.zeros((CG, 128, 128), np.float32)
    spread = np.zeros((128, CG, 128), np.float32)
    eye = np.eye(KX, dtype=np.float32)
    for o in range(CG):
        for i in range(CG):
            gather[o, i * KX : (i + 1) * KX, o * KX : (o + 1) * KX] = eye
            spread[o * KX : (o + 1) * KX, o, i * KX : (i + 1) * KX] = eye
    return gather.reshape(CG * 128, 128), spread.reshape(128, CG * 128)


def mm(a, b):
    return jnp.dot(a, b, preferred_element_type=F32)


def split(v):
    high = v.astype(BF16)
    return high, (v - high.astype(F32)).astype(BF16)


def call(body, outs, *args, scratch=(), mib=12):
    return pl.pallas_call(
        body,
        out_shape=outs,
        scratch_shapes=list(scratch),
        compiler_params=pltpu.CompilerParams(vmem_limit_bytes=mib * 2**20),
    )(*args)


def shape(*dims, dtype=F32):
    return jax.ShapeDtypeStruct(dims, dtype)


def far(*values):
    return [pltpu.with_memory_space_constraint(v, pltpu.HBM) for v in values]


def halves_of_rows(core, x):
    own = pl.ds(pl.multiple_of(x * 80 + core * 40, 8), 40)
    other = pl.ds(pl.multiple_of(x * 80 + (1 - core) * 40, 8), 40)
    return own, other


def part_with(core, c_ref, keep_ref, send_ref):
    late = []
    for x in range(XL):
        own, other = halves_of_rows(core, x)
        keep_ref[0, x * 40 : x * 40 + 40, :] = c_ref[0, own, :]
        keep_ref[1, x * 40 : x * 40 + 40, :] = c_ref[1, own, :]
        send_ref[x * 40 : x * 40 + 40, :] = c_ref[0, other, :]
        late.append(c_ref[1, other, :][:, :64])
    for x in range(XL // 2):
        send_ref[KEEP + x * 40 : KEEP + x * 40 + 40, :] = jnp.concatenate([late[x], late[x + XL // 2]], axis=1)


def join(core, keep_ref, recv_ref, g_ref):
    for x in range(XL):
        own, other = halves_of_rows(core, x)
        g_ref[0, own, :] = keep_ref[0, x * 40 : x * 40 + 40, :]
        g_ref[1, own, :] = keep_ref[1, x * 40 : x * 40 + 40, :]
        g_ref[0, other, :] = recv_ref[x * 40 : x * 40 + 40, :]
    for x in range(XL // 2):
        both = recv_ref[KEEP + x * 40 : KEEP + x * 40 + 40, :]
        for h in range(2):
            g_ref[1, halves_of_rows(core, x + h * XL // 2)[1], :64] = both[:, h * 64 : h * 64 + 64]


def load_tables(me_ref, high_hbm, low_hbm, high_ref, low_ref, sems):
    me = me_ref[0]
    copies = [
        pltpu.make_async_copy(high_hbm.at[me], high_ref, sems.at[0]),
        pltpu.make_async_copy(low_hbm.at[me], low_ref, sems.at[1]),
    ]
    for copy in copies:
        copy.start()
    return copies


def contract_kernel(me_ref, keep_ref, recv_ref, high_hbm, low_hbm, o_ref, high_ref, low_ref, sems):
    copies = load_tables(me_ref, high_hbm, low_hbm, high_ref, low_ref, sems)
    rows = []
    for y in range(YL):
        both = recv_ref[pl.ds(KEEP + y, HC // 2, stride=YL), :]
        first = jnp.concatenate(
            [keep_ref[0, pl.ds(y, HC, stride=YL), :], recv_ref[pl.ds(y, HC, stride=YL), :]], axis=0
        )
        second = jnp.concatenate(
            [keep_ref[1, pl.ds(y, HC, stride=YL), :][:, :64], both[:, :64], both[:, 64:]], axis=0
        )
        rows += [first.T, second.T]
    vh, vl = split(jnp.concatenate(rows, axis=0))
    for copy in copies:
        copy.wait()
    p = mm(vh, high_ref[...]) + (mm(vl, high_ref[...]) + mm(vh, low_ref[...]))
    for y in range(YL):
        for m in range(ML):
            at = y * N + m * GY
            re, im = p[at : at + GY], p[at + N // 2 : at + N // 2 + GY]
            parts = (re[:, :256] + im[:, 256:], im[:, :256] - re[:, 256:])
            for part in range(2):
                for g in range(2):
                    o_ref[pl.ds((m * 2 + g) * 8 + part * YL + y, GY, stride=CHUNK), :] = parts[part][
                        :, g * 128 : (g + 1) * 128
                    ]


def expand_kernel(me_ref, r_ref, high_hbm, low_hbm, keep_ref, send_ref, high_ref, low_ref, sems):
    copies = load_tables(me_ref, high_hbm, low_hbm, high_ref, low_ref, sems)
    rows = []
    for y in range(YL):
        for part in range(2):
            for m in range(ML):
                rows.append(
                    jnp.concatenate(
                        [
                            r_ref[pl.ds((m * 2 + g) * 8 + part * YL + y, GY, stride=CHUNK), :]
                            for g in range(2)
                        ],
                        axis=1,
                    )
                )
    vh, vl = split(jnp.concatenate(rows, axis=0))
    for copy in copies:
        copy.wait()
    p = mm(vh, high_ref[...]) + (mm(vl, high_ref[...]) + mm(vh, low_ref[...]))
    for y in range(YL):
        re, im = p[y * N : y * N + N // 2], p[y * N + N // 2 : y * N + N]
        real = re[:, :XC] - im[:, 384 : 384 + XC]
        imag = re[:, 384 : 384 + XC] + im[:, :XC]
        first = jnp.concatenate([real, imag[:GY]], axis=0).T
        second = imag[GY:].T
        keep_ref[0, pl.ds(y, HC, stride=YL), :] = first[:HC]
        keep_ref[1, pl.ds(y, HC, stride=YL), :] = jnp.concatenate(
            [second[:HC], jnp.zeros((HC, 64), F32)], axis=1
        )
        send_ref[pl.ds(y, HC, stride=YL), :] = first[HC:]
        send_ref[pl.ds(KEEP + y, HC // 2, stride=YL), :] = jnp.concatenate(
            [second[HC : HC + HC // 2], second[HC + HC // 2 :]], axis=1
        )


def analyze_kernel(me_ref, f_ref, table_ref, keep_ref, send_ref, c_ref, v_ref, t_ref, sems):
    table = pltpu.make_async_copy(table_ref, t_ref, sems.at[4])
    table.start()
    copies = [pltpu.make_async_copy(f_ref.at[pl.ds(i * 4, 4)], v_ref.at[pl.ds(i * 4, 4)], sems.at[i]) for i in range(4)]
    for copy in copies:
        copy.start()
    table.wait()
    for i in range(4):
        copies[i].wait()
        v = jnp.concatenate([v_ref[i * 4 + k].reshape(C * YL, Q) for k in range(4)], axis=0)
        r = mm(v, t_ref[...])
        c_ref[0, i * 320 : (i + 1) * 320, :] = r[:, :128]
        c_ref[1, i * 320 : (i + 1) * 320, :64] = r[:, 128:]
    part_with(me_ref[0] % 2, c_ref, keep_ref, send_ref)


def widen(table, e_ref, et_ref, mask_ref):
    tall = mm(e_ref[...], table).astype(BF16)
    return mm(tall, et_ref[...]).astype(BF16) * mask_ref[...]


def linear_kernel(f_ref, d_ref, w_ref, b_ref, e_ref, et_ref, mask_ref, lin_ref, row_ref):
    mix = widen(w_ref[...], e_ref, et_ref, mask_ref)
    bias = jnp.sum(e_ref[...].astype(F32) * b_ref[...], axis=1, keepdims=True)

    def body(i, _):
        x = 2 * i
        rows = pl.ds(pl.multiple_of(i * 160, 16), 160)
        fv = jnp.concatenate([f_ref[x + h].reshape(C * YL, Q) for h in range(2)], axis=0)
        lin_ref[rows, :] = mm(mix, fv) + bias
        row_ref[rows, :] = jnp.concatenate([d_ref[x + h].reshape(C * YL, Q) for h in range(2)], axis=0)
        return 0

    lax.fori_loop(0, XL // 2, body, 0)


def linear_back_kernel(p_ref, w_ref, e_ref, et_ref, mask_ref, lin_ref):
    mix = widen(w_ref[...], e_ref, et_ref, mask_ref)

    def body(i, _):
        rows = pl.ds(pl.multiple_of(i * 160, 16), 160)
        lin_ref[rows, :] = mm(mix, p_ref[rows, :])
        return 0

    lax.fori_loop(0, XL // 2, body, 0)


def synthesis_rows(g_ref, rows):
    gh0, gl0 = split(g_ref[0, rows, :])
    gh1, gl1 = split(g_ref[1, rows, :])
    gh1, gl1 = gh1[:, :64], gl1[:, :64]
    return jnp.concatenate([gh0, gh1, gl0, gl1, gh0, gh1], axis=1)


def pieces(source, target, sems):
    return [
        pltpu.make_async_copy(source.at[pl.ds(i * n, n)], target.at[pl.ds(i * n, n)], sems.at[i])
        for n in [source.shape[0] // 4]
        for i in range(4)
    ]


def forward_kernel(
    me_ref, keep_ref, recv_ref, lin_ref, d_hbm, s_ref, t_ref, out_hbm, pre_hbm, keep_out, send_ref,
    g_ref, c_ref, d_ref, sp_ref, out_ref, pre_ref, sems,
):
    d_in = pieces(d_hbm, d_ref, sems.at[2])
    for copy in d_in:
        copy.start()
    out_out, pre_out = pieces(out_ref, out_hbm, sems.at[0]), pieces(pre_ref, pre_hbm, sems.at[1])
    core = me_ref[0] % 2
    join(core, keep_ref, recv_ref, g_ref)
    for i in range(4):
        rows = slice(i * 320, (i + 1) * 320)
        sp_ref[...] = mm(synthesis_rows(g_ref, rows), s_ref[...])
        d_in[i].wait()

        def body(k, _, i=i):
            at = pl.ds(pl.multiple_of(i * 320 + k * 80, 16), 80)
            before = sp_ref[pl.ds(pl.multiple_of(k * 80, 16), 80), :] + lin_ref[at, :]
            square = before * before
            tangent = jnp.tanh(before * (GELU_SCALE + (GELU_SCALE * GELU_CUBIC) * square))
            half = 0.5 + 0.5 * tangent
            result = before * half
            slope = half + result * (1.0 - tangent) * (GELU_SCALE + (3.0 * GELU_SCALE * GELU_CUBIC) * square)
            pre_ref[at, :] = (d_ref[at, :].astype(F32) * slope).astype(BF16)
            out_ref[i * 4 + k] = result.astype(BF16).reshape(C, YL, Q)
            return 0

        lax.fori_loop(0, 4, body, 0)
        out_out[i].start()
        pre_out[i].start()
        r = mm(pre_ref[rows, :], t_ref[...])
        c_ref[0, rows, :] = r[:, :128]
        c_ref[1, rows, :64] = r[:, 128:]
    part_with(core, c_ref, keep_out, send_ref)
    for i in range(4):
        out_out[i].wait()
        pre_out[i].wait()


def backward_kernel(me_ref, keep_ref, recv_ref, lin_ref, s_ref, out_hbm, g_ref, sp_ref, out_ref, sems):
    out_out = pieces(out_ref, out_hbm, sems)
    join(me_ref[0] % 2, keep_ref, recv_ref, g_ref)
    for i in range(4):
        rows = slice(i * 320, (i + 1) * 320)
        sp_ref[...] = mm(synthesis_rows(g_ref, rows), s_ref[...])
        for k in range(4):
            total = sp_ref[k * 80 : (k + 1) * 80, :] + lin_ref[i * 320 + k * 80 : i * 320 + (k + 1) * 80, :]
            out_ref[i * 4 + k] = total.astype(BF16).reshape(C, YL, Q)
        out_out[i].start()
    for i in range(4):
        out_out[i].wait()


def inward_kernel(r_ref, yh_ref, yl_ref, o_ref):
    columns = []
    for lt in range(LT):
        columns.append(
            jnp.concatenate([r_ref[pl.ds(lt * 8 + k, GY, stride=CHUNK), :] for k in range(8)], axis=0)
        )
    vh, vl = split(jnp.concatenate(columns, axis=1))
    p = mm(yh_ref[...], vh) + (mm(yh_ref[...], vl) + mm(yl_ref[...], vh))
    for lt in range(LT):
        m, g = divmod(lt, 2)
        for part in range(2):
            for ky in range(KYL):
                o_ref[pl.ds(g * 18 + part * 9 + ky * ML + m, GX, stride=XROWS), :] = p[
                    part * 24 + ky * 8 : part * 24 + ky * 8 + 8, lt * 128 : (lt + 1) * 128
                ]


def outward_kernel(z_ref, y_ref, o_ref):
    columns = []
    for lt in range(LT):
        m, g = divmod(lt, 2)
        columns.append(
            jnp.concatenate(
                [
                    z_ref[pl.ds(g * 18 + part * 9 + ky * ML + m, GX, stride=XROWS), :]
                    for part in range(2)
                    for ky in range(KYL)
                ],
                axis=0,
            )
        )
    vh, vl = split(jnp.concatenate(columns, axis=1))
    o = mm(y_ref[...], jnp.concatenate([vh, vl, vh], axis=0))
    for lt in range(LT):
        for k in range(8):
            o_ref[pl.ds(lt * 8 + k, GY, stride=CHUNK), :] = o[k * GY : (k + 1) * GY, lt * 128 : (lt + 1) * 128]


def part_rows(ref, g, part):
    return ref[g * 18 + part * 9 : g * 18 + part * 9 + 9, :]


def send_all(o_ref, r_ref):
    for a in range(GX):
        core = a % 2
        o_ref[a * XROWS : (a + 1) * XROWS, :] = r_ref[core * XROWS : (core + 1) * XROWS, :]


def sum_chips(q_ref, core):
    return sum(q_ref[a * XROWS : (a + 1) * XROWS, :] for a in range(core, GX, 2))


def mix_kernel(q_ref, w_ref, e_ref, u_ref, o_ref, l_ref, r_ref):
    for core in range(2):
        u_ref[core * XROWS : (core + 1) * XROWS, :] = sum_chips(q_ref, core)
    us = [[part_rows(u_ref, g, part) for part in range(2)] for g in range(G)]
    l_ref[...] = jnp.zeros_like(l_ref)
    for o in range(C):
        real = imag = None
        for g in range(G):
            wr, wi = w_ref[o, g, 0], w_ref[o, g, 1]
            ur, ui = us[g]
            a, b = wr * ur - wi * ui, wr * ui + wi * ur
            real, imag = (a, b) if real is None else (real + a, imag + b)
        gi, oi = divmod(o, CG)
        l_ref[gi * 32 : gi * 32 + 9, oi * 128 : (oi + 1) * 128] = real
        l_ref[gi * 32 + 16 : gi * 32 + 25, oi * 128 : (oi + 1) * 128] = imag
    vh, vl = split(l_ref[...])
    v = (mm(vh, e_ref[...]) + mm(vl, e_ref[...])) * SCALE
    for g in range(G):
        for part in range(2):
            r_ref[g * 18 + part * 9 : g * 18 + part * 9 + 9, :] = v[g * 32 + part * 16 : g * 32 + part * 16 + 9]
    send_all(o_ref, r_ref)


def unmix_kernel(q_ref, w_ref, e_ref, s_ref, o_ref, l_ref, r_ref):
    for core in range(2):
        r_ref[core * XROWS : (core + 1) * XROWS, :] = sum_chips(q_ref, core) * SCALE
    l_ref[...] = jnp.zeros_like(l_ref)
    for g in range(G):
        for part in range(2):
            l_ref[g * 32 + part * 16 : g * 32 + part * 16 + 9, :] = part_rows(r_ref, g, part)
    vh, vl = split(l_ref[...])
    s_ref[...] = mm(vh, e_ref[...]) + mm(vl, e_ref[...])
    acc = [[None, None] for _ in range(G)]
    for o in range(C):
        gi, oi = divmod(o, CG)
        gr = s_ref[gi * 32 : gi * 32 + 9, oi * 128 : (oi + 1) * 128]
        gm = s_ref[gi * 32 + 16 : gi * 32 + 25, oi * 128 : (oi + 1) * 128]
        for g in range(G):
            wr, wi = w_ref[o, g, 0], w_ref[o, g, 1]
            a, b = wr * gr + wi * gm, wr * gm - wi * gr
            acc[g] = [a, b] if acc[g][0] is None else [acc[g][0] + a, acc[g][1] + b]
    for g in range(G):
        for part in range(2):
            r_ref[g * 18 + part * 9 : g * 18 + part * 9 + 9, :] = acc[g][part]
    send_all(o_ref, r_ref)


def outer_kernel(u_ref, s_ref, o_ref):
    us = [[part_rows(u_ref, g, part) for part in range(2)] for g in range(G)]
    for o in range(C):
        gi, oi = divmod(o, CG)
        gr = s_ref[gi * 32 : gi * 32 + 9, oi * 128 : (oi + 1) * 128]
        gm = s_ref[gi * 32 + 16 : gi * 32 + 25, oi * 128 : (oi + 1) * 128]
        for g in range(G):
            ur, ui = us[g]
            o_ref[o, g, 0] = gr * ur + gm * ui
            o_ref[o, g, 1] = gm * ur - gr * ui


def per_device(field, cotangent, spectral_weight, pointwise_weight, channel_bias):
    analysis, synthesis = zt_tables()
    toward = jnp.asarray(analysis.astype(jnp.bfloat16))
    toward_back = jnp.asarray(synthesis.astype(jnp.bfloat16))
    outward = jnp.asarray(three_rows(synthesis.T))
    outward_back = jnp.asarray(three_rows(analysis.T))
    ytab = y_table()
    y_in = [jnp.asarray(t) for t in halves(ytab)]
    yh, yl = halves(ytab.T)
    y_out = jnp.asarray(np.concatenate([yh, yh, yl], axis=1))
    xtab, xturned = x_tables()
    x_in = [jnp.asarray(t) for t in halves(xtab)]
    x_out = [jnp.asarray(t) for t in halves(xturned)]
    me = jnp.full((1,), lax.axis_index("gx"), jnp.int32)
    gather, spread = group_tables()
    gather, spread = jnp.asarray(gather.astype(jnp.bfloat16)), jnp.asarray(spread.astype(jnp.bfloat16))
    f = jnp.transpose(field, (0, 2, 1, 3))
    d = jnp.transpose(cotangent, (0, 2, 1, 3))
    row_channel = (np.arange(160) // YL) % C
    pick = (row_channel[:, None] == np.arange(C)[None, :]).astype(jnp.bfloat16)
    cell = (np.arange(160) // (C * YL)) * YL + np.arange(160) % YL
    wide = [jnp.asarray(v) for v in (pick, pick.T, (cell[:, None] == cell[None, :]).astype(jnp.bfloat16))]
    w = spectral_weight.reshape(2, G, CG, C, KX, KYL, ML)
    w = jnp.transpose(w, (3, 1, 0, 5, 6, 2, 4)).reshape(C, G, 2, MODES, KC)
    w = jnp.pad(w, ((0, 0),) * 4 + ((0, 128 - KC),))

    hbm, vmem = pl.BlockSpec(memory_space=pltpu.HBM), pl.BlockSpec(memory_space=pltpu.VMEM)
    smem = pl.BlockSpec(memory_space=pltpu.SMEM)

    def over_y(v):
        return lax.all_to_all(v.reshape(GY, 1, CHUNK * 128), "gy", split_axis=0, concat_axis=0, tiled=True).reshape(
            GY * CHUNK, 128
        )

    def over_x(v):
        return lax.all_to_all(v.reshape(GX, 1, XROWS * 128), "gx", split_axis=0, concat_axis=0, tiled=True).reshape(
            GX * XROWS, 128
        )

    def swap(v):
        return lax.ppermute(v, "gx", [(a, a ^ 1) for a in range(GX)])

    def kernel(body, outs, in_specs, *args, scratch, mib, out_specs=vmem):
        return pl.pallas_call(
            body,
            out_shape=outs,
            in_specs=in_specs,
            out_specs=out_specs,
            scratch_shapes=scratch,
            compiler_params=pltpu.CompilerParams(vmem_limit_bytes=mib * 2**20),
        )(*args)

    def contract(keep, send):
        return kernel(
            contract_kernel, shape(GY * CHUNK, 128), [smem, vmem, vmem, hbm, hbm],
            me, keep, swap(send), *far(*x_in), mib=16,
            scratch=[pltpu.VMEM((XC, 512), BF16)] * 2 + [pltpu.SemaphoreType.DMA((2,))],
        )

    def expand(v):
        keep, send = kernel(
            expand_kernel, (shape(2, KEEP, 128), shape(SWAP, 128)), [smem, vmem, hbm, hbm],
            me, v, *far(*x_out), mib=16, out_specs=(vmem, vmem),
            scratch=[pltpu.VMEM((256, 768), BF16)] * 2 + [pltpu.SemaphoreType.DMA((2,))],
        )
        return keep, swap(send)

    def outward_part(v):
        return call(outward_kernel, shape(GY * CHUNK, 128), over_x(v), y_out)

    cells = pltpu.VMEM((2, CELLS, 128), F32)
    rows = pltpu.VMEM((ROWS, 128), F32)
    part = pltpu.VMEM((320, Q), F32)
    full16 = pltpu.VMEM((CELLS, Q), BF16)
    native = pltpu.VMEM((XL, C, YL, Q), BF16)
    grid, grid16 = pltpu.HBM((CELLS, Q), F32), pltpu.HBM((CELLS, Q), BF16)
    kept, sent = shape(2, KEEP, 128), shape(SWAP, 128)
    keep, send = kernel(
        analyze_kernel, (kept, sent), [smem, hbm, hbm], me, *far(f, toward), mib=16, out_specs=(vmem, vmem),
        scratch=[cells, native, pltpu.VMEM((Q, N), BF16), pltpu.SemaphoreType.DMA((5,))],
    )
    v, w = lax.optimization_barrier((over_y(contract(keep, send)), w))
    v = call(inward_kernel, shape(GX * XROWS, 128), v, *y_in)
    u, v = call(
        mix_kernel, (shape(ROWS, 128), shape(GX * XROWS, 128)), over_x(v), w, gather,
        scratch=[pltpu.VMEM((128, CG * 128), F32), rows],
    )
    v, f, d = lax.optimization_barrier((outward_part(v), f, d))
    lin, d = call(
        linear_kernel, (grid, grid16), f, d, pointwise_weight.T, channel_bias.reshape(1, C), *wide, mib=18
    )
    v, lin, d = lax.optimization_barrier((over_y(v), lin, d))
    output, pre, keep, send = kernel(
        forward_kernel, (shape(XL, C, YL, Q, dtype=BF16), grid16, kept, sent), [smem] + [vmem] * 3 + [hbm, vmem, vmem],
        me, *expand(v), lin, *far(d), outward, toward_back, mib=28, out_specs=(hbm, hbm, vmem, vmem),
        scratch=[cells, cells, full16, part, native, full16, pltpu.SemaphoreType.DMA((3, 4))],
    )
    v = call(inward_kernel, shape(GX * XROWS, 128), over_y(contract(keep, send)), *y_in)
    s, v = call(
        unmix_kernel, (shape(128, CG * 128), shape(GX * XROWS, 128)), over_x(v), w, spread,
        scratch=[pltpu.VMEM((128, 128), F32), rows],
    )
    v, s, pre = lax.optimization_barrier((outward_part(v), s, pre))
    lin = call(linear_back_kernel, grid, pre, pointwise_weight, *wide, mib=14)
    gw = call(outer_kernel, shape(C, G, 2, MODES, 128), u, s)
    gw = gw[..., :KC].reshape(C, G, 2, KYL, ML, CG, KX)
    grad_weight = jnp.transpose(gw, (2, 1, 5, 0, 6, 3, 4)).reshape(2, C, C, KX, KYL, ML)
    v, lin, grad_weight = lax.optimization_barrier((over_y(v), lin, grad_weight))
    grad_field = kernel(
        backward_kernel, shape(XL, C, YL, Q, dtype=BF16), [smem] + [vmem] * 4,
        me, *expand(v), lin, outward_back, mib=18, out_specs=hbm,
        scratch=[cells, part, native, pltpu.SemaphoreType.DMA((4,))],
    )
    return (jnp.transpose(output, (0, 2, 1, 3)), jnp.transpose(grad_field, (0, 2, 1, 3)), grad_weight)


def solution(mesh):
    grid = P("gx", "gy", None, None)
    modes = P(None, None, None, None, "gx", "gy")
    return jax.shard_map(
        per_device,
        mesh=mesh,
        in_specs=(grid, grid, modes, P(), P()),
        out_specs=(grid, grid, modes),
        check_vma=False,
    )
```

```python
import math

import jax
import jax.numpy as jnp
import numpy as np
from jax import lax
from jax.experimental import pallas as pl
from jax.experimental.pallas import tpu as pltpu
from jax.sharding import PartitionSpec as P

NX = 128
NY = 128
NZ = 64
NT = 16
C = 20
KX = 24
KY = 24
KZ = 12
KT = 8

GX = 8
GY = 32
XL = NX // GX
YL = NY // GY
KYL = KY // GX
ML = KZ * KT // GY
XC = XL * C
CELLS = XL * C * YL
Q = NZ * NT
N = 2 * ML * GY
HALF = C // 2
HC = XL * HALF
KEEP = HC * YL
SWAP = KEEP * 3 // 2
LT = 6
WHOLE = 5
CHUNK = WHOLE * 8 + 5
G = 4
CG = C // G
KC = CG * KX
MODES = KYL * ML
ROWS = G * 2 * MODES
XROWS = ROWS // 2

GELU_SCALE = math.sqrt(2.0 / math.pi)
GELU_CUBIC = 0.044715
F32 = jnp.float32
BF16 = jnp.bfloat16
SCALE = 1.0 / (NX * NY)


def signed(count):
    j = np.arange(count)
    return np.where(j < count // 2, j, j - count)


def halves(table):
    table = np.asarray(table, np.float32)
    high = table.astype(jnp.bfloat16)
    low = (table - high.astype(np.float32)).astype(jnp.bfloat16)
    return high, low


def zt_tables():
    q = np.arange(Q)
    m = (np.arange(GY)[None, :] * ML + np.arange(ML)[:, None]).reshape(-1)
    fz, kt = signed(KZ)[m // KT], m % KT
    phase = (fz[None, :] * (q // NT)[:, None] * NT + kt[None, :] * (q % NT)[:, None] * NZ) % Q
    angles = phase * (2.0 * math.pi / Q)
    weights = np.where(kt == 0, 1.0, 2.0) / Q
    analysis = np.concatenate([np.cos(angles), -np.sin(angles)], axis=1)
    synthesis = analysis * np.concatenate([weights, weights])[None, :]
    return analysis.astype(np.float32), synthesis.astype(np.float32)


def three_rows(table):
    high, low = halves(table)
    return np.concatenate([high, high, low], axis=0)


def y_table():
    ky = (np.arange(GX)[None, :] * KYL + np.arange(KYL)[:, None]).reshape(-1)
    f = signed(KY)[ky]
    n = np.arange(NY)
    angles = ((f[:, None] * n[None, :]) % NY) * (2.0 * math.pi / NY)
    c, s = np.cos(angles), np.sin(angles)
    t = np.zeros((2, KY, GY, 2, YL))
    c4, s4 = c.reshape(KY, GY, YL), s.reshape(KY, GY, YL)
    t[0, :, :, 0], t[0, :, :, 1] = c4, s4
    t[1, :, :, 0], t[1, :, :, 1] = -s4, c4
    return np.transpose(t, (0, 1, 3, 4, 2)).reshape(2 * KY, 2 * YL * GY)


def x_tables():
    f = signed(KX)
    t = np.zeros((GX, 2, XL, HALF, 2, 2, 128))
    for a in range(GX):
        for side in range(2):
            cells = XL * (a ^ side) + np.arange(XL)
            angles = ((f[None, :] * cells[:, None]) % NX) * (2.0 * math.pi / NX)
            for c in range(HALF):
                g, j = divmod(c, CG)
                t[a, side, :, c, 0, g, j * KX : (j + 1) * KX] = np.cos(angles)
                t[a, side, :, c, 1, g, j * KX : (j + 1) * KX] = np.sin(angles)
    turned = np.zeros((GX, 256, 2, 384))
    turned[..., :XC] = np.transpose(t, (0, 5, 6, 4, 1, 2, 3)).reshape(GX, 256, 2, XC)
    turned = turned.reshape(GX, 2, 128, 768)[:, :, :KC].reshape(GX, 2 * KC, 768)
    return t.reshape(GX, XC, 512), turned


def group_tables():
    gather = np.zeros((CG, 128, 128), np.float32)
    spread = np.zeros((128, CG, 128), np.float32)
    eye = np.eye(KX, dtype=np.float32)
    for o in range(CG):
        for i in range(CG):
            gather[o, i * KX : (i + 1) * KX, o * KX : (o + 1) * KX] = eye
            spread[o * KX : (o + 1) * KX, o, i * KX : (i + 1) * KX] = eye
    return gather.reshape(CG * 128, 128), spread.reshape(128, CG * 128)


def mm(a, b):
    return jnp.dot(a, b, preferred_element_type=F32)


def split(v):
    high = v.astype(BF16)
    return high, (v - high.astype(F32)).astype(BF16)


def call(body, outs, *args, scratch=(), mib=12):
    return pl.pallas_call(
        body,
        out_shape=outs,
        scratch_shapes=list(scratch),
        compiler_params=pltpu.CompilerParams(vmem_limit_bytes=mib * 2**20),
    )(*args)


def shape(*dims, dtype=F32):
    return jax.ShapeDtypeStruct(dims, dtype)


def far(*values):
    return [pltpu.with_memory_space_constraint(v, pltpu.HBM) for v in values]


def halves_of_rows(core, x):
    own = pl.ds(pl.multiple_of(x * 80 + core * 40, 8), 40)
    other = pl.ds(pl.multiple_of(x * 80 + (1 - core) * 40, 8), 40)
    return own, other


def part_with(core, c_ref, keep_ref, send_ref):
    late = []
    for x in range(XL):
        own, other = halves_of_rows(core, x)
        keep_ref[0, x * 40 : x * 40 + 40, :] = c_ref[0, own, :]
        keep_ref[1, x * 40 : x * 40 + 40, :] = c_ref[1, own, :]
        send_ref[x * 40 : x * 40 + 40, :] = c_ref[0, other, :]
        late.append(c_ref[1, other, :][:, :64])
    for x in range(XL // 2):
        send_ref[KEEP + x * 40 : KEEP + x * 40 + 40, :] = jnp.concatenate([late[x], late[x + XL // 2]], axis=1)


def join(core, keep_ref, recv_ref, g_ref):
    for x in range(XL):
        own, other = halves_of_rows(core, x)
        g_ref[0, own, :] = keep_ref[0, x * 40 : x * 40 + 40, :]
        g_ref[1, own, :] = keep_ref[1, x * 40 : x * 40 + 40, :]
        g_ref[0, other, :] = recv_ref[x * 40 : x * 40 + 40, :]
    for x in range(XL // 2):
        both = recv_ref[KEEP + x * 40 : KEEP + x * 40 + 40, :]
        for h in range(2):
            g_ref[1, halves_of_rows(core, x + h * XL // 2)[1], :64] = both[:, h * 64 : h * 64 + 64]


def store_rest(o_ref, rests):
    for j in range(4):
        o_ref[pl.ds(WHOLE * 8 + j, GY, stride=CHUNK), :] = jnp.concatenate(
            [rests[2 * j][:, :64], rests[2 * j + 1][:, :64]], axis=1
        )
    o_ref[pl.ds(WHOLE * 8 + 4, GY, stride=CHUNK), :] = jnp.concatenate([r[:, 64:80] for r in rests], axis=1)


def load_rest(r_ref):
    halves_of_tiles = [r_ref[pl.ds(WHOLE * 8 + j, GY, stride=CHUNK), :] for j in range(4)]
    last = r_ref[pl.ds(WHOLE * 8 + 4, GY, stride=CHUNK), :]
    return [
        jnp.concatenate(
            [halves_of_tiles[k // 2][:, k % 2 * 64 : k % 2 * 64 + 64], last[:, k * 16 : k * 16 + 16]], axis=1
        )
        for k in range(8)
    ]


def load_tables(me_ref, high_hbm, low_hbm, high_ref, low_ref, sems):
    me = me_ref[0]
    copies = [
        pltpu.make_async_copy(high_hbm.at[me], high_ref, sems.at[0]),
        pltpu.make_async_copy(low_hbm.at[me], low_ref, sems.at[1]),
    ]
    for copy in copies:
        copy.start()
    return copies


def contract_kernel(me_ref, keep_ref, recv_ref, high_hbm, low_hbm, o_ref, high_ref, low_ref, sems):
    copies = load_tables(me_ref, high_hbm, low_hbm, high_ref, low_ref, sems)
    rows = []
    for y in range(YL):
        both = recv_ref[pl.ds(KEEP + y, HC // 2, stride=YL), :]
        first = jnp.concatenate(
            [keep_ref[0, pl.ds(y, HC, stride=YL), :], recv_ref[pl.ds(y, HC, stride=YL), :]], axis=0
        )
        second = jnp.concatenate(
            [keep_ref[1, pl.ds(y, HC, stride=YL), :][:, :64], both[:, :64], both[:, 64:]], axis=0
        )
        rows += [first.T, second.T]
    vh, vl = split(jnp.concatenate(rows, axis=0))
    for copy in copies:
        copy.wait()
    p = mm(vh, high_ref[...]) + (mm(vl, high_ref[...]) + mm(vh, low_ref[...]))
    rests = [None] * 8
    for y in range(YL):
        lanes = ([], [])
        for m in range(ML):
            at = y * N + m * GY
            re, im = p[at : at + GY], p[at + N // 2 : at + N // 2 + GY]
            parts = (re[:, :256] + im[:, 256:], im[:, :256] - re[:, 256:])
            for part in range(2):
                lanes[part].extend(parts[part][:, g * 128 : g * 128 + KC] for g in range(2))
        for part in range(2):
            row = jnp.concatenate(lanes[part], axis=1)
            for lt in range(WHOLE):
                o_ref[pl.ds(lt * 8 + part * YL + y, GY, stride=CHUNK), :] = row[:, lt * 128 : (lt + 1) * 128]
            rests[part * YL + y] = row[:, WHOLE * 128 :]
    store_rest(o_ref, rests)


def expand_kernel(me_ref, r_ref, high_hbm, low_hbm, keep_ref, send_ref, high_ref, low_ref, sems):
    copies = load_tables(me_ref, high_hbm, low_hbm, high_ref, low_ref, sems)
    rows = []
    rests = load_rest(r_ref)
    for y in range(YL):
        for part in range(2):
            k = part * YL + y
            row = jnp.concatenate(
                [r_ref[pl.ds(lt * 8 + k, GY, stride=CHUNK), :] for lt in range(WHOLE)] + [rests[k]], axis=1
            )
            rows += [row[:, m * 2 * KC : (m + 1) * 2 * KC] for m in range(ML)]
    vh, vl = split(jnp.concatenate(rows, axis=0))
    for copy in copies:
        copy.wait()
    p = mm(vh, high_ref[...]) + (mm(vl, high_ref[...]) + mm(vh, low_ref[...]))
    for y in range(YL):
        re, im = p[y * N : y * N + N // 2], p[y * N + N // 2 : y * N + N]
        real = re[:, :XC] - im[:, 384 : 384 + XC]
        imag = re[:, 384 : 384 + XC] + im[:, :XC]
        first = jnp.concatenate([real, imag[:GY]], axis=0).T
        second = imag[GY:].T
        keep_ref[0, pl.ds(y, HC, stride=YL), :] = first[:HC]
        keep_ref[1, pl.ds(y, HC, stride=YL), :] = jnp.concatenate(
            [second[:HC], jnp.zeros((HC, 64), F32)], axis=1
        )
        send_ref[pl.ds(y, HC, stride=YL), :] = first[HC:]
        send_ref[pl.ds(KEEP + y, HC // 2, stride=YL), :] = jnp.concatenate(
            [second[HC : HC + HC // 2], second[HC + HC // 2 :]], axis=1
        )


def analyze_kernel(me_ref, f_ref, table_ref, keep_ref, send_ref, c_ref, v_ref, t_ref, sems):
    table = pltpu.make_async_copy(table_ref, t_ref, sems.at[4])
    table.start()
    copies = [pltpu.make_async_copy(f_ref.at[pl.ds(i * 4, 4)], v_ref.at[pl.ds(i * 4, 4)], sems.at[i]) for i in range(4)]
    for copy in copies:
        copy.start()
    table.wait()
    for i in range(4):
        copies[i].wait()
        v = jnp.concatenate([v_ref[i * 4 + k].reshape(C * YL, Q) for k in range(4)], axis=0)
        r = mm(v, t_ref[...])
        c_ref[0, i * 320 : (i + 1) * 320, :] = r[:, :128]
        c_ref[1, i * 320 : (i + 1) * 320, :64] = r[:, 128:]
    part_with(me_ref[0] % 2, c_ref, keep_ref, send_ref)


def widen(table, e_ref, et_ref, mask_ref):
    tall = mm(e_ref[...], table).astype(BF16)
    return mm(tall, et_ref[...]).astype(BF16) * mask_ref[...]


def linear_kernel(f_ref, d_ref, w_ref, b_ref, e_ref, et_ref, mask_ref, lin_ref, row_ref):
    mix = widen(w_ref[...], e_ref, et_ref, mask_ref)
    bias = jnp.sum(e_ref[...].astype(F32) * b_ref[...], axis=1, keepdims=True)

    def body(i, _):
        x = 2 * i
        rows = pl.ds(pl.multiple_of(i * 160, 16), 160)
        fv = jnp.concatenate([f_ref[x + h].reshape(C * YL, Q) for h in range(2)], axis=0)
        lin_ref[rows, :] = mm(mix, fv) + bias
        row_ref[rows, :] = jnp.concatenate([d_ref[x + h].reshape(C * YL, Q) for h in range(2)], axis=0)
        return 0

    lax.fori_loop(0, XL // 2, body, 0)


def linear_back_kernel(p_ref, w_ref, e_ref, et_ref, mask_ref, lin_ref):
    mix = widen(w_ref[...], e_ref, et_ref, mask_ref)

    def body(i, _):
        rows = pl.ds(pl.multiple_of(i * 160, 16), 160)
        lin_ref[rows, :] = mm(mix, p_ref[rows, :])
        return 0

    lax.fori_loop(0, XL // 2, body, 0)


def synthesis_rows(g_ref, rows):
    gh0, gl0 = split(g_ref[0, rows, :])
    gh1, gl1 = split(g_ref[1, rows, :])
    gh1, gl1 = gh1[:, :64], gl1[:, :64]
    return jnp.concatenate([gh0, gh1, gl0, gl1, gh0, gh1], axis=1)


def pieces(source, target, sems):
    return [
        pltpu.make_async_copy(source.at[pl.ds(i * n, n)], target.at[pl.ds(i * n, n)], sems.at[i])
        for n in [source.shape[0] // 4]
        for i in range(4)
    ]


def forward_kernel(
    me_ref, keep_ref, recv_ref, lin_ref, d_hbm, s_ref, t_ref, out_hbm, pre_hbm, keep_out, send_ref,
    g_ref, c_ref, d_ref, sp_ref, out_ref, pre_ref, sems,
):
    d_in = pieces(d_hbm, d_ref, sems.at[2])
    for copy in d_in:
        copy.start()
    out_out, pre_out = pieces(out_ref, out_hbm, sems.at[0]), pieces(pre_ref, pre_hbm, sems.at[1])
    core = me_ref[0] % 2
    join(core, keep_ref, recv_ref, g_ref)
    for i in range(4):
        rows = slice(i * 320, (i + 1) * 320)
        sp_ref[...] = mm(synthesis_rows(g_ref, rows), s_ref[...])
        d_in[i].wait()

        def body(k, _, i=i):
            at = pl.ds(pl.multiple_of(i * 320 + k * 80, 16), 80)
            before = sp_ref[pl.ds(pl.multiple_of(k * 80, 16), 80), :] + lin_ref[at, :]
            square = before * before
            tangent = jnp.tanh(before * (GELU_SCALE + (GELU_SCALE * GELU_CUBIC) * square))
            half = 0.5 + 0.5 * tangent
            result = before * half
            slope = half + result * (1.0 - tangent) * (GELU_SCALE + (3.0 * GELU_SCALE * GELU_CUBIC) * square)
            pre_ref[at, :] = (d_ref[at, :].astype(F32) * slope).astype(BF16)
            out_ref[i * 4 + k] = result.astype(BF16).reshape(C, YL, Q)
            return 0

        lax.fori_loop(0, 4, body, 0)
        out_out[i].start()
        pre_out[i].start()
        r = mm(pre_ref[rows, :], t_ref[...])
        c_ref[0, rows, :] = r[:, :128]
        c_ref[1, rows, :64] = r[:, 128:]
    part_with(core, c_ref, keep_out, send_ref)
    for i in range(4):
        out_out[i].wait()
        pre_out[i].wait()


def backward_kernel(me_ref, keep_ref, recv_ref, lin_ref, s_ref, out_hbm, g_ref, sp_ref, out_ref, sems):
    out_out = pieces(out_ref, out_hbm, sems)
    join(me_ref[0] % 2, keep_ref, recv_ref, g_ref)
    for i in range(4):
        rows = slice(i * 320, (i + 1) * 320)
        sp_ref[...] = mm(synthesis_rows(g_ref, rows), s_ref[...])
        for k in range(4):
            total = sp_ref[k * 80 : (k + 1) * 80, :] + lin_ref[i * 320 + k * 80 : i * 320 + (k + 1) * 80, :]
            out_ref[i * 4 + k] = total.astype(BF16).reshape(C, YL, Q)
        out_out[i].start()
    for i in range(4):
        out_out[i].wait()


def inward_kernel(r_ref, yh_ref, yl_ref, o_ref):
    columns = [
        jnp.concatenate([r_ref[pl.ds(lt * 8 + k, GY, stride=CHUNK), :] for k in range(8)], axis=0)
        for lt in range(WHOLE)
    ]
    columns.append(jnp.concatenate(load_rest(r_ref), axis=0))
    vh, vl = split(jnp.concatenate(columns, axis=1))
    p = mm(yh_ref[...], vh) + (mm(yh_ref[...], vl) + mm(yl_ref[...], vh))
    blank = jnp.zeros((2 * KY, 128 - KC), F32)
    for lt in range(LT):
        m, g = divmod(lt, 2)
        tile = jnp.concatenate([p[:, lt * KC : (lt + 1) * KC], blank], axis=1)
        for part in range(2):
            for ky in range(KYL):
                o_ref[pl.ds(g * 18 + part * 9 + ky * ML + m, GX, stride=XROWS), :] = tile[
                    part * 24 + ky * 8 : part * 24 + ky * 8 + 8
                ]


def outward_kernel(z_ref, y_ref, o_ref):
    columns = []
    for lt in range(LT):
        m, g = divmod(lt, 2)
        columns.append(
            jnp.concatenate(
                [
                    z_ref[pl.ds(g * 18 + part * 9 + ky * ML + m, GX, stride=XROWS), :]
                    for part in range(2)
                    for ky in range(KYL)
                ],
                axis=0,
            )[:, :KC]
        )
    vh, vl = split(jnp.concatenate(columns, axis=1))
    o = mm(y_ref[...], jnp.concatenate([vh, vl, vh], axis=0))
    for k in range(8):
        for lt in range(WHOLE):
            o_ref[pl.ds(lt * 8 + k, GY, stride=CHUNK), :] = o[k * GY : (k + 1) * GY, lt * 128 : (lt + 1) * 128]
    store_rest(o_ref, [o[k * GY : (k + 1) * GY, WHOLE * 128 :] for k in range(8)])


def part_rows(ref, g, part):
    return ref[g * 18 + part * 9 : g * 18 + part * 9 + 9, :]


def send_all(o_ref, r_ref):
    for a in range(GX):
        core = a % 2
        o_ref[a * XROWS : (a + 1) * XROWS, :] = r_ref[core * XROWS : (core + 1) * XROWS, :]


def sum_chips(q_ref, core):
    return sum(q_ref[a * XROWS : (a + 1) * XROWS, :] for a in range(core, GX, 2))


def mix_kernel(q_ref, w_ref, e_ref, u_ref, o_ref, l_ref, r_ref):
    for core in range(2):
        u_ref[core * XROWS : (core + 1) * XROWS, :] = sum_chips(q_ref, core)
    us = [[part_rows(u_ref, g, part) for part in range(2)] for g in range(G)]
    l_ref[...] = jnp.zeros_like(l_ref)
    for o in range(C):
        real = imag = None
        for g in range(G):
            wr, wi = w_ref[o, g, 0], w_ref[o, g, 1]
            ur, ui = us[g]
            a, b = wr * ur - wi * ui, wr * ui + wi * ur
            real, imag = (a, b) if real is None else (real + a, imag + b)
        gi, oi = divmod(o, CG)
        l_ref[gi * 32 : gi * 32 + 9, oi * 128 : (oi + 1) * 128] = real
        l_ref[gi * 32 + 16 : gi * 32 + 25, oi * 128 : (oi + 1) * 128] = imag
    vh, vl = split(l_ref[...])
    v = (mm(vh, e_ref[...]) + mm(vl, e_ref[...])) * SCALE
    for g in range(G):
        for part in range(2):
            r_ref[g * 18 + part * 9 : g * 18 + part * 9 + 9, :] = v[g * 32 + part * 16 : g * 32 + part * 16 + 9]
    send_all(o_ref, r_ref)


def unmix_kernel(q_ref, w_ref, e_ref, s_ref, o_ref, l_ref, r_ref):
    for core in range(2):
        r_ref[core * XROWS : (core + 1) * XROWS, :] = sum_chips(q_ref, core) * SCALE
    l_ref[...] = jnp.zeros_like(l_ref)
    for g in range(G):
        for part in range(2):
            l_ref[g * 32 + part * 16 : g * 32 + part * 16 + 9, :] = part_rows(r_ref, g, part)
    vh, vl = split(l_ref[...])
    s_ref[...] = mm(vh, e_ref[...]) + mm(vl, e_ref[...])
    acc = [[None, None] for _ in range(G)]
    for o in range(C):
        gi, oi = divmod(o, CG)
        gr = s_ref[gi * 32 : gi * 32 + 9, oi * 128 : (oi + 1) * 128]
        gm = s_ref[gi * 32 + 16 : gi * 32 + 25, oi * 128 : (oi + 1) * 128]
        for g in range(G):
            wr, wi = w_ref[o, g, 0], w_ref[o, g, 1]
            a, b = wr * gr + wi * gm, wr * gm - wi * gr
            acc[g] = [a, b] if acc[g][0] is None else [acc[g][0] + a, acc[g][1] + b]
    for g in range(G):
        for part in range(2):
            r_ref[g * 18 + part * 9 : g * 18 + part * 9 + 9, :] = acc[g][part]
    send_all(o_ref, r_ref)


def outer_kernel(u_ref, s_ref, o_ref):
    us = [[part_rows(u_ref, g, part) for part in range(2)] for g in range(G)]
    for o in range(C):
        gi, oi = divmod(o, CG)
        gr = s_ref[gi * 32 : gi * 32 + 9, oi * 128 : (oi + 1) * 128]
        gm = s_ref[gi * 32 + 16 : gi * 32 + 25, oi * 128 : (oi + 1) * 128]
        for g in range(G):
            ur, ui = us[g]
            o_ref[o, g, 0] = gr * ur + gm * ui
            o_ref[o, g, 1] = gm * ur - gr * ui


def per_device(field, cotangent, spectral_weight, pointwise_weight, channel_bias):
    analysis, synthesis = zt_tables()
    toward = jnp.asarray(analysis.astype(jnp.bfloat16))
    toward_back = jnp.asarray(synthesis.astype(jnp.bfloat16))
    outward = jnp.asarray(three_rows(synthesis.T))
    outward_back = jnp.asarray(three_rows(analysis.T))
    ytab = y_table()
    y_in = [jnp.asarray(t) for t in halves(ytab)]
    yh, yl = halves(ytab.T)
    y_out = jnp.asarray(np.concatenate([yh, yh, yl], axis=1))
    xtab, xturned = x_tables()
    x_in = [jnp.asarray(t) for t in halves(xtab)]
    x_out = [jnp.asarray(t) for t in halves(xturned)]
    me = jnp.full((1,), lax.axis_index("gx"), jnp.int32)
    gather, spread = group_tables()
    gather, spread = jnp.asarray(gather.astype(jnp.bfloat16)), jnp.asarray(spread.astype(jnp.bfloat16))
    f = jnp.transpose(field, (0, 2, 1, 3))
    d = jnp.transpose(cotangent, (0, 2, 1, 3))
    row_channel = (np.arange(160) // YL) % C
    pick = (row_channel[:, None] == np.arange(C)[None, :]).astype(jnp.bfloat16)
    cell = (np.arange(160) // (C * YL)) * YL + np.arange(160) % YL
    wide = [jnp.asarray(v) for v in (pick, pick.T, (cell[:, None] == cell[None, :]).astype(jnp.bfloat16))]
    w = spectral_weight.reshape(2, G, CG, C, KX, KYL, ML)
    w = jnp.transpose(w, (3, 1, 0, 5, 6, 2, 4)).reshape(C, G, 2, MODES, KC)
    w = jnp.pad(w, ((0, 0),) * 4 + ((0, 128 - KC),))

    hbm, vmem = pl.BlockSpec(memory_space=pltpu.HBM), pl.BlockSpec(memory_space=pltpu.VMEM)
    smem = pl.BlockSpec(memory_space=pltpu.SMEM)

    def over_y(v):
        return lax.all_to_all(v.reshape(GY, 1, CHUNK * 128), "gy", split_axis=0, concat_axis=0, tiled=True).reshape(
            GY * CHUNK, 128
        )

    def over_x(v):
        return lax.all_to_all(v.reshape(GX, 1, XROWS * 128), "gx", split_axis=0, concat_axis=0, tiled=True).reshape(
            GX * XROWS, 128
        )

    def swap(v):
        return lax.ppermute(v, "gx", [(a, a ^ 1) for a in range(GX)])

    def kernel(body, outs, in_specs, *args, scratch, mib, out_specs=vmem):
        return pl.pallas_call(
            body,
            out_shape=outs,
            in_specs=in_specs,
            out_specs=out_specs,
            scratch_shapes=scratch,
            compiler_params=pltpu.CompilerParams(vmem_limit_bytes=mib * 2**20),
        )(*args)

    def contract(keep, send):
        return kernel(
            contract_kernel, shape(GY * CHUNK, 128), [smem, vmem, vmem, hbm, hbm],
            me, keep, swap(send), *far(*x_in), mib=16,
            scratch=[pltpu.VMEM((XC, 512), BF16)] * 2 + [pltpu.SemaphoreType.DMA((2,))],
        )

    def expand(v):
        keep, send = kernel(
            expand_kernel, (shape(2, KEEP, 128), shape(SWAP, 128)), [smem, vmem, hbm, hbm],
            me, v, *far(*x_out), mib=16, out_specs=(vmem, vmem),
            scratch=[pltpu.VMEM((2 * KC, 768), BF16)] * 2 + [pltpu.SemaphoreType.DMA((2,))],
        )
        return keep, swap(send)

    def outward_part(v):
        return call(outward_kernel, shape(GY * CHUNK, 128), over_x(v), y_out)

    cells = pltpu.VMEM((2, CELLS, 128), F32)
    rows = pltpu.VMEM((ROWS, 128), F32)
    part = pltpu.VMEM((320, Q), F32)
    full16 = pltpu.VMEM((CELLS, Q), BF16)
    native = pltpu.VMEM((XL, C, YL, Q), BF16)
    grid, grid16 = pltpu.HBM((CELLS, Q), F32), pltpu.HBM((CELLS, Q), BF16)
    kept, sent = shape(2, KEEP, 128), shape(SWAP, 128)
    keep, send = kernel(
        analyze_kernel, (kept, sent), [smem, hbm, hbm], me, *far(f, toward), mib=16, out_specs=(vmem, vmem),
        scratch=[cells, native, pltpu.VMEM((Q, N), BF16), pltpu.SemaphoreType.DMA((5,))],
    )
    v, w = lax.optimization_barrier((over_y(contract(keep, send)), w))
    v = call(inward_kernel, shape(GX * XROWS, 128), v, *y_in)
    u, v = call(
        mix_kernel, (shape(ROWS, 128), shape(GX * XROWS, 128)), over_x(v), w, gather,
        scratch=[pltpu.VMEM((128, CG * 128), F32), rows],
    )
    v, f, d = lax.optimization_barrier((outward_part(v), f, d))
    lin, d = call(
        linear_kernel, (grid, grid16), f, d, pointwise_weight.T, channel_bias.reshape(1, C), *wide, mib=18
    )
    v, lin, d = lax.optimization_barrier((over_y(v), lin, d))
    output, pre, keep, send = kernel(
        forward_kernel, (shape(XL, C, YL, Q, dtype=BF16), grid16, kept, sent), [smem] + [vmem] * 3 + [hbm, vmem, vmem],
        me, *expand(v), lin, *far(d), outward, toward_back, mib=28, out_specs=(hbm, hbm, vmem, vmem),
        scratch=[cells, cells, full16, part, native, full16, pltpu.SemaphoreType.DMA((3, 4))],
    )
    v = call(inward_kernel, shape(GX * XROWS, 128), over_y(contract(keep, send)), *y_in)
    s, v = call(
        unmix_kernel, (shape(128, CG * 128), shape(GX * XROWS, 128)), over_x(v), w, spread,
        scratch=[pltpu.VMEM((128, 128), F32), rows],
    )
    v, s, pre = lax.optimization_barrier((outward_part(v), s, pre))
    lin = call(linear_back_kernel, grid, pre, pointwise_weight, *wide, mib=14)
    gw = call(outer_kernel, shape(C, G, 2, MODES, 128), u, s)
    gw = gw[..., :KC].reshape(C, G, 2, KYL, ML, CG, KX)
    grad_weight = jnp.transpose(gw, (2, 1, 5, 0, 6, 3, 4)).reshape(2, C, C, KX, KYL, ML)
    v, lin, grad_weight = lax.optimization_barrier((over_y(v), lin, grad_weight))
    grad_field = kernel(
        backward_kernel, shape(XL, C, YL, Q, dtype=BF16), [smem] + [vmem] * 4,
        me, *expand(v), lin, outward_back, mib=18, out_specs=hbm,
        scratch=[cells, part, native, pltpu.SemaphoreType.DMA((4,))],
    )
    return (jnp.transpose(output, (0, 2, 1, 3)), jnp.transpose(grad_field, (0, 2, 1, 3)), grad_weight)


def solution(mesh):
    grid = P("gx", "gy", None, None)
    modes = P(None, None, None, None, "gx", "gy")
    return jax.shard_map(
        per_device,
        mesh=mesh,
        in_specs=(grid, grid, modes, P(), P()),
        out_specs=(grid, grid, modes),
        check_vma=False,
    )
```
